512 devices in a mesh: seq: 64 (over z_lo, y, core), tp: 8 (over z_hi, x).
Axes of the slice: x: 4, y: 8, z: 8 (z_hi: 2, z_lo: 4; z = z_hi * 4 + z_lo), core: 2. Of those that a mesh axis runs over, the one named last changes fastest.
Arguments:
- queries: bfloat16 [16384, 4096], P('seq', 'tp'), may hold values from -64 to 64
- keys: bfloat16 [16384, 1024], P('seq', 'tp'), may hold values from -6 to 6
- values: bfloat16 [16384, 1024], P('seq', 'tp'), may hold values from -6 to 6
- key_head_scale: float32 [8], P('tp'), may hold values from 0.5 to 2
- retained: int32 [64, 1], P('seq'), may hold values from 0 to 1
- out_weight: bfloat16 [4096, 4096], P('tp'), may hold values from -0.09375 to 0.09375
- norm_gain: float32 [4096], P('tp'), may hold values from 0.5 to 1.5
Outputs:
- normed: bfloat16 [16384, 4096], P('seq', 'tp')
The draws below stay inside these ranges and needn't reach their ends.
All inputs are finite; a program needn't handle non-finite values.
Results may differ from the reference program's by a relative error of at most 0.02.
Values may be sent and summed in bfloat16 or wider, within the bound.
No kernel may reach another device: no remote copies, remote signals or barrier semaphores. Data moves between devices by JAX's collectives and lax.ppermute only.
A program may use at most 128 MiB of HBM per device.

```python
import math
import jax
import jax.numpy as jnp
from jax import lax

D = 4096
QUERY_HEAD_COUNT = 32
KEY_VALUE_HEADS = 8
HEAD_WIDTH = 128
KEY_BLOCK_TOKENS = 128
KEEP = 1
INDEX_TOKENS = 256
SEQUENCE_TOKENS = 16384
N_SEQ = 64
N_TP = 8


def shared_keys(key):
    sampled_numbers = jax.random.normal(jax.random.fold_in(key, 11), (SEQUENCE_TOKENS, KEY_VALUE_HEADS * HEAD_WIDTH), jnp.float32)
    return jnp.clip(sampled_numbers, -6.0, 6.0)


def draw_keys(key, part):
    drawn_key_rows = shared_keys(key)
    return drawn_key_rows.astype(jnp.bfloat16)


def draw_queries(key, part):
    key = jax.random.fold_in(key, 2)
    sampled_numbers = jnp.clip(jax.random.normal(key, (SEQUENCE_TOKENS, QUERY_HEAD_COUNT * HEAD_WIDTH), jnp.float32), -6.0, 6.0)
    return jnp.clip(sampled_numbers, -64.0, 64.0).astype(jnp.bfloat16)


def with_ends(values, key, smallest, high):
    spot = [jax.random.randint(jax.random.fold_in(key, axis), (), 0, length) for axis, length in enumerate(values.shape)]
    main_axis = values.shape.index(max(values.shape))
    beside = spot[:main_axis] + [(spot[main_axis] + 1) % values.shape[main_axis]] + spot[main_axis + 1:]
    return values.at[tuple(spot)].set(smallest).at[tuple(beside)].set(high)


def steps_of(stream_key, extent, shards, least, largest):
    loudness = 1.0
    for axis_at, parts in shards:
        steps = jax.random.uniform(jax.random.fold_in(jax.random.fold_in(stream_key, 6), axis_at), (parts,), jnp.float32, least / len(shards), largest / len(shards))
        loudness = loudness * jnp.repeat(jnp.exp(steps), extent[axis_at] // parts).reshape((-1,) + (1,) * (len(extent) - 1 - axis_at))
    return loudness


def gaussian(own_key, shape, spread, limit, pieces=(), held_as=jnp.bfloat16):
    drawn = spread * jax.random.normal(own_key, shape, jnp.float32)
    if pieces:
        drawn = drawn * steps_of(own_key, shape, pieces, -0.22, 0.18)
    return jnp.clip(drawn, -limit, limit).astype(held_as)


def setup_inputs(seed: int = 0) -> dict:
    seeds = jax.random.split(jax.random.key(seed), 8)
    return {
        "queries": draw_queries(jax.random.fold_in(seeds[7], 71), 0),
        "keys": draw_keys(jax.random.fold_in(seeds[7], 71), 0),
        "values": gaussian(seeds[2], (SEQUENCE_TOKENS, KEY_VALUE_HEADS * HEAD_WIDTH), 1.0, 6.0, ((0, 64), (1, 8))),
        "key_head_scale": jnp.clip(jnp.exp(math.log(2.0) - 1.3862944 * jax.random.uniform(seeds[3], (KEY_VALUE_HEADS,), jnp.float32) ** steps_of(seeds[3], (KEY_VALUE_HEADS,), ((0, 8),), -0.2, 0.2)), 0.5, 2.0),
        "retained": with_ends(jax.random.randint(seeds[4], (N_SEQ, KEEP), 0, INDEX_TOKENS // KEY_BLOCK_TOKENS), jax.random.fold_in(seeds[4], 1), 0, (INDEX_TOKENS // KEY_BLOCK_TOKENS) - 1).astype(jnp.int32),
        "out_weight": gaussian(seeds[5], (QUERY_HEAD_COUNT * HEAD_WIDTH, D), (QUERY_HEAD_COUNT * HEAD_WIDTH) ** -0.5, 0.09375, ((0, 8),)),
        "norm_gain": jnp.clip(1.0 + 0.1 * jax.random.normal(seeds[6], (D,), jnp.float32), 0.5, 1.5),
    }


def reference(queries, keys, values, key_head_scale, retained, out_weight, norm_gain):
    query_group_count = QUERY_HEAD_COUNT // KEY_VALUE_HEADS
    block_rows = jnp.arange(N_SEQ, dtype=jnp.int32)[:, None] * INDEX_TOKENS + retained * KEY_BLOCK_TOKENS
    passed_rows = (block_rows[:, :, None] + jnp.arange(KEY_BLOCK_TOKENS, dtype=jnp.int32)[None, None, :]).reshape(-1)
    owner_dev = jnp.repeat(jnp.arange(N_SEQ, dtype=jnp.int32), KEEP * KEY_BLOCK_TOKENS)
    received_keys = keys[passed_rows]
    received_values = values[passed_rows]
    causal = jnp.arange(INDEX_TOKENS)[:, None] >= jnp.arange(INDEX_TOKENS)[None, :]
    group_cols = QUERY_HEAD_COUNT * HEAD_WIDTH // N_TP

    def one_piece(device):
        leading_row = (device * INDEX_TOKENS).astype(jnp.int32)
        local_query = lax.dynamic_slice_in_dim(queries, leading_row, INDEX_TOKENS, 0).astype(jnp.float32).reshape(INDEX_TOKENS, KEY_VALUE_HEADS, query_group_count, HEAD_WIDTH)
        local_keys = lax.dynamic_slice_in_dim(keys, leading_row, INDEX_TOKENS, 0)
        local_values = lax.dynamic_slice_in_dim(values, leading_row, INDEX_TOKENS, 0)
        gathered_keys = jnp.concatenate([keys[:KEY_BLOCK_TOKENS], received_keys, local_keys], 0).astype(jnp.float32).reshape(-1, KEY_VALUE_HEADS, HEAD_WIDTH)
        gathered_values = jnp.concatenate([values[:KEY_BLOCK_TOKENS], received_values, local_values], 0).astype(jnp.float32).reshape(-1, KEY_VALUE_HEADS, HEAD_WIDTH)
        anchor_mask = jnp.broadcast_to(device > 0, (INDEX_TOKENS, KEY_BLOCK_TOKENS))
        passed_mask = jnp.broadcast_to((owner_dev < device)[None, :], (INDEX_TOKENS, owner_dev.shape[0]))
        visible = jnp.concatenate([anchor_mask, passed_mask, causal], 1)[:, None, None, :]
        scores = jnp.einsum('chgd,khd->chgk', local_query, gathered_keys) * (key_head_scale / math.sqrt(HEAD_WIDTH))[None, :, None, None]
        row_max = lax.optimization_barrier(jnp.max(jnp.where(visible, scores, -1e+30), -1))
        weights = jnp.where(visible, jnp.exp(scores - row_max[..., None]), 0.0)
        denominator = lax.optimization_barrier(jnp.sum(weights, -1))
        rounded = lax.optimization_barrier(weights.astype(jnp.bfloat16)).astype(jnp.float32)
        attended = jnp.einsum('chgk,khd->chgd', rounded, gathered_values) / denominator[..., None]
        attended = attended.reshape(INDEX_TOKENS, QUERY_HEAD_COUNT * HEAD_WIDTH).astype(jnp.bfloat16)
        projected = jnp.zeros((INDEX_TOKENS, D), jnp.float32)
        for group in range(N_TP):
            partial_sum = jnp.dot(attended[:, group * group_cols:(group + 1) * group_cols], out_weight[group * group_cols:(group + 1) * group_cols], preferred_element_type=jnp.float32)
            projected = projected + lax.optimization_barrier(partial_sum.astype(jnp.bfloat16)).astype(jnp.float32)
        mean_square = lax.optimization_barrier(jnp.mean(projected * projected, -1, keepdims=True))
        return (projected / jnp.sqrt(mean_square + 1e-05) * norm_gain[None, :]).astype(jnp.bfloat16)
    result = lax.map(one_piece, jnp.arange(N_SEQ, dtype=jnp.int32))
    return result.reshape(SEQUENCE_TOKENS, D)
```

```python
import functools
import math

import jax
import jax.numpy as jnp
from jax import lax
from jax.experimental import pallas as pl
from jax.experimental.pallas import tpu as pltpu
from jax.sharding import PartitionSpec as P

HEAD = 128
BLOCK = 128
LOG2E = math.log2(math.e)
NZ, NY, NC = 4, 8, 2
NX, NH = 4, 2
HEADS = 4
TOK = 256
SLOT = 2 * BLOCK
MSG = NZ * SLOT
LOW = -1e30
F32 = jnp.float32
BF16 = jnp.bfloat16

SMEM = pl.BlockSpec(memory_space=pltpu.SMEM)
VMEM = pl.BlockSpec(memory_space=pltpu.VMEM)
M_SHAPE = jax.ShapeDtypeStruct((HEADS, TOK, HEAD), F32)
ACC_SHAPE = jax.ShapeDtypeStruct((HEADS, TOK, 2 * HEAD), F32)


def sid(z, y, c):
    return (z * NY + y % NY) * NC + c


PLACES = [(z, y, c) for z in range(NZ) for y in range(NY) for c in range(NC)]
LAST = sid(NZ - 1, NY - 1, 1)


def z_perm(k):
    pairs = [(sid(z, y, c), sid(z + k, y, c)) for z, y, c in PLACES if z + k < NZ]
    return pairs + [(LAST, sid(k - 1, NY - 1, 1))]


def y_perm(k):
    return [(sid(z, y, c), sid(z, y + k, c)) for z, y, c in PLACES]


def cross(a, b):
    return lax.dot_general(a, b, (((1,), (1,)), ((), ())), preferred_element_type=F32)


def plain(a, b):
    return lax.dot_general(a, b, (((1,), (0,)), ((), ())), preferred_element_type=F32)


def wide(a, n):
    return jnp.concatenate([a] * n, axis=1)


def seen(me, query_core, key_y):
    z, y, core = me // (NY * NC), (me // NC) % NY, me % NC
    anchor = jnp.logical_and(core == 1, key_y == NY - 1)
    first_piece = (z * NY + y) * NC + query_core == 0
    below = jnp.logical_or(key_y < y, jnp.logical_and(key_y == y, core < query_core))
    own = jnp.where(anchor, jnp.logical_not(first_piece).astype(jnp.int32), below.astype(jnp.int32))
    return [own] + [(z >= k).astype(jnp.int32) for k in range(1, NZ)]


def prepare(blocks, shown, kk, vv):
    first = jnp.int32(0)
    for j in reversed(range(len(shown))):
        first = jnp.where(shown[j] > 0, j, first)
    for j, flag in enumerate(shown):
        src = jnp.where(flag > 0, j, first)
        rows = pl.multiple_of(src * SLOT, SLOT)
        kk[pl.ds(j * BLOCK, BLOCK), :] = blocks[pl.ds(rows, BLOCK), :]
        scale = flag.astype(F32)
        v = blocks[pl.ds(j * SLOT + BLOCK, BLOCK), :].astype(F32) * scale
        vv[pl.ds(j * BLOCK, BLOCK), 0:HEAD] = v.astype(BF16)
        vv[pl.ds(j * BLOCK, BLOCK), HEAD : 2 * HEAD] = jnp.full((BLOCK, HEAD), scale, F32).astype(BF16)


def update(c, q, kk, vv, m_ref, acc_ref, h):
    s = cross(q, kk[...]) * c
    m_old = m_ref[h]
    m_new = jnp.maximum(m_old, jnp.max(s, axis=1, keepdims=True))
    alpha = jnp.exp2(m_old - m_new)
    p = jnp.exp2(s - wide(m_new, s.shape[1] // HEAD)).astype(BF16)
    acc_ref[h] = acc_ref[h] * wide(alpha, 2) + plain(p, vv[...])
    m_ref[h] = m_new


def attend_set(me, core, key_ys, c, q_ref, blocks, kk, vv, m_ref, acc_ref):
    shown = []
    for key_y in key_ys:
        shown += seen(me, core, key_y)
    total = functools.reduce(lambda a, b: a + b, shown)

    @pl.when(total > 0)
    def _():
        prepare(blocks, shown, kk, vv)
        for h in range(HEADS):
            update(c, q_ref[:, h * HEAD : (h + 1) * HEAD], kk, vv, m_ref, acc_ref, h)


def first_kernel(me_ref, c_ref, q0, q1, k_ref, v_ref, blk, m0, a0, m1, a1, blocks, kk, vv, lv):
    me = me_ref[0]
    c = c_ref[0]
    core = me % NC
    lv[:, 0:HEAD] = v_ref[...]
    lv[:, HEAD : 2 * HEAD] = jnp.ones((TOK, HEAD), BF16)
    row = lax.broadcasted_iota(jnp.int32, (TOK, TOK), 0)
    col = lax.broadcasted_iota(jnp.int32, (TOK, TOK), 1)
    for h in range(HEADS):
        s = cross(q0[:, h * HEAD : (h + 1) * HEAD], k_ref[...]) * c
        s = jnp.where(row >= col, s, LOW)
        m = jnp.broadcast_to(jnp.max(s, axis=1, keepdims=True), (TOK, HEAD))
        p = jnp.exp2(s - wide(m, TOK // HEAD)).astype(BF16)
        a0[h] = plain(p, lv[...])
        m0[h] = m
        m1[h] = jnp.full((TOK, HEAD), LOW, F32)
        a1[h] = jnp.zeros((TOK, 2 * HEAD), F32)
    blocks[...] = blk[...]
    y = (me // NC) % NY
    attend_set(me, core, [y], c, q0, blocks, kk, vv, m0, a0)
    attend_set(me, 1 - core, [y], c, q1, blocks, kk, vv, m1, a1)


def ring_kernel(step, me_ref, c_ref, q0, q1, fwd, bwd, m0i, a0i, m1i, a1i, m0, a0, m1, a1, blocks, kk, vv):
    me = me_ref[0]
    c = c_ref[0]
    core = me % NC
    y = (me // NC) % NY
    m0[...] = m0i[...]
    a0[...] = a0i[...]
    m1[...] = m1i[...]
    a1[...] = a1i[...]
    blocks[0:MSG, :] = fwd[...]
    blocks[MSG : 2 * MSG, :] = bwd[...]
    key_ys = [(y + NY - step) % NY, (y + step) % NY]
    attend_set(me, core, key_ys, c, q0, blocks, kk, vv, m0, a0)
    attend_set(me, 1 - core, key_ys, c, q1, blocks, kk, vv, m1, a1)


def last_kernel(other, me_ref, c_ref, q, blk, mi, ai, *rest):
    if other:
        out, m, a, kk, vv = rest
    else:
        m, a, kk, vv = rest
    me = me_ref[0]
    core = me % NC
    y = (me // NC) % NY
    m[...] = mi[...]
    a[...] = ai[...]
    key_ys = [(y + NY // 2) % NY]
    attend_set(me, 1 - core if other else core, key_ys, c_ref[0], q, blk, kk, vv, m, a)
    if other:
        lane = lax.broadcasted_iota(jnp.int32, (TOK, HEAD), 1)
        for h in range(HEADS):
            total = a[h][:, HEAD:]
            some = total > 0.0
            safe = jnp.where(some, total, 1.0)
            out[h, :, 0:HEAD] = (a[h][:, :HEAD] / safe).astype(BF16)
            lse = jnp.where(some, m[h] + jnp.log2(safe), LOW)
            hi = lse.astype(BF16).astype(F32)
            mid = (lse - hi).astype(BF16).astype(F32)
            low = lse - hi - mid
            parts = jnp.where(lane == 0, hi, jnp.where(lane == 1, mid, low))
            out[h, :, HEAD : 2 * HEAD] = parts.astype(BF16)


def merge_kernel(tp_ref, m, a, got, w, att, out):
    @pl.when(pl.program_id(0) == 0)
    def _():
        for h in range(HEADS):
            parts = got[h][:, HEAD:].astype(F32)
            lse = (parts[:, 0:1] + parts[:, 1:2]) + parts[:, 2:3]
            mine = m[h]
            top = jnp.maximum(mine, lse)
            w0 = jnp.exp2(mine - top)
            w1 = jnp.exp2(lse - top)
            acc = a[h][:, :HEAD] * w0 + got[h][:, :HEAD].astype(F32) * w1
            total = a[h][:, HEAD:] * w0 + w1
            att[:, h * HEAD : (h + 1) * HEAD] = (acc / total).astype(BF16)

    out[0] = plain(att[...], w[...]).astype(BF16)


def rest_kernel(tp_ref, att, w, out):
    out[0] = plain(att[...], w[...]).astype(BF16)


def params(mib=48):
    return pltpu.CompilerParams(vmem_limit_bytes=mib << 20)


def scratch(n):
    return [pltpu.VMEM((n * BLOCK, HEAD), BF16), pltpu.VMEM((n * BLOCK, 2 * HEAD), BF16)]


def cost(keys, sets):
    rows = HEADS * TOK * sets
    return pl.CostEstimate(
        flops=rows * keys * HEAD * 6, bytes_accessed=4 << 20, transcendentals=rows * keys
    )


def shards(queries, keys, values, key_head_scale, retained, out_weight, norm_gain):
    me = lax.axis_index("seq").astype(jnp.int32)
    tp = lax.axis_index("tp").astype(jnp.int32)
    core, y, z = me % NC, (me // NC) % NY, me // (NC * NY)
    hi = tp // NX
    me_s = me.reshape(1)
    tp_s = tp.reshape(1)
    c = key_head_scale * (LOG2E / math.sqrt(HEAD))

    anchor = jnp.concatenate([keys[:BLOCK], values[:BLOCK]], 0)
    anchor_far = lax.ppermute(anchor, "seq", [(0, LAST)])
    other_queries = lax.ppermute(queries, "seq", [(sid(*s), sid(s[0], s[1], 1 - s[2])) for s in PLACES])
    row = retained[0, 0] * BLOCK
    own = jnp.concatenate(
        [
            lax.dynamic_slice_in_dim(keys, row, BLOCK, 0),
            lax.dynamic_slice_in_dim(values, row, BLOCK, 0),
        ],
        0,
    )
    own = jnp.where(me == LAST, anchor_far, own)
    up = [lax.ppermute(own, "seq", z_perm(k)) for k in range(1, NZ)]
    far = jnp.where(z == 0, up[0], jnp.where(z == 1, up[1], jnp.where(z == 2, up[2], own)))
    slot = jnp.where(jnp.logical_and(y == NY - 1, core == 1), far, own)
    block = jnp.concatenate([slot] + up, 0)

    fwd = [lax.ppermute(block, "seq", y_perm(1))]
    bwd = [lax.ppermute(block, "seq", y_perm(-1))]
    for _ in range(2):
        fwd.append(lax.ppermute(fwd[-1], "seq", y_perm(1)))
        bwd.append(lax.ppermute(bwd[-1], "seq", y_perm(-1)))
    turn = [(sid(z_, y_, c_), sid(z_, y_ + (1 if c_ == 0 else -1), c_)) for z_, y_, c_ in PLACES]
    half = lax.ppermute(jnp.where(core == 0, fwd[-1], bwd[-1]), "seq", turn)

    state_shapes = [M_SHAPE, ACC_SHAPE, M_SHAPE, ACC_SHAPE]
    state = pl.pallas_call(
        first_kernel,
        out_shape=state_shapes,
        in_specs=[SMEM, SMEM] + [VMEM] * 5,
        out_specs=[VMEM] * 4,
        scratch_shapes=[pltpu.VMEM((MSG, HEAD), BF16)] + scratch(4) + [pltpu.VMEM((TOK, 2 * HEAD), BF16)],
        compiler_params=params(),
        cost_estimate=cost(640, 2),
        name="attend_own_chip",
    )(me_s, c, queries, other_queries, keys, values, block)
    for step in range(1, 4):
        state = pl.pallas_call(
            functools.partial(ring_kernel, step),
            out_shape=state_shapes,
            in_specs=[SMEM, SMEM] + [VMEM] * 8,
            out_specs=[VMEM] * 4,
            scratch_shapes=[pltpu.VMEM((2 * MSG, HEAD), BF16)] + scratch(8),
            input_output_aliases={6: 0, 7: 1, 8: 2, 9: 3},
            compiler_params=params(),
            cost_estimate=cost(1024, 2),
            name="attend_ring",
        )(me_s, c, queries, other_queries, fwd[step - 1], bwd[step - 1], *state)
    m0, a0, m1, a1 = state
    message, _, _ = pl.pallas_call(
        functools.partial(last_kernel, True),
        out_shape=[jax.ShapeDtypeStruct((HEADS, TOK, 2 * HEAD), BF16), M_SHAPE, ACC_SHAPE],
        in_specs=[SMEM, SMEM] + [VMEM] * 4,
        out_specs=[VMEM] * 3,
        scratch_shapes=scratch(4),
        input_output_aliases={4: 1, 5: 2},
        compiler_params=params(),
        cost_estimate=cost(512, 1),
        name="attend_last_other",
    )(me_s, c, other_queries, half, m1, a1)
    got = lax.ppermute(message, "seq", [(sid(*s), sid(s[0], s[1], 1 - s[2])) for s in PLACES])
    m0, a0 = pl.pallas_call(
        functools.partial(last_kernel, False),
        out_shape=[M_SHAPE, ACC_SHAPE],
        in_specs=[SMEM, SMEM] + [VMEM] * 4,
        out_specs=[VMEM] * 2,
        scratch_shapes=scratch(4),
        input_output_aliases={4: 0, 5: 1},
        compiler_params=params(),
        cost_estimate=cost(512, 1),
        name="attend_last_own",
    )(me_s, c, queries, half, m0, a0)

    wide_cols = out_weight.shape[1] // (NX * NH)

    def far_cols(i, tp_ref):
        return (0, i * NX + (tp_ref[0] + 2) % NX)

    def rest_cols(i, tp_ref):
        g = i // 2
        d = jnp.where(g == 2, 0, 1 + 2 * g)
        return (0, (i % 2) * NX + (tp_ref[0] + d) % NX)

    whole = lambda *shape: pl.BlockSpec(shape, lambda i, tp_ref: (0,) * len(shape))
    att, far_part = pl.pallas_call(
        merge_kernel,
        out_shape=[
            jax.ShapeDtypeStruct((TOK, HEADS * HEAD), BF16),
            jax.ShapeDtypeStruct((2, TOK, wide_cols), BF16),
        ],
        grid_spec=pltpu.PrefetchScalarGridSpec(
            num_scalar_prefetch=1,
            grid=(2,),
            in_specs=[
                whole(HEADS, TOK, HEAD),
                whole(HEADS, TOK, 2 * HEAD),
                whole(HEADS, TOK, 2 * HEAD),
                pl.BlockSpec((HEADS * HEAD, wide_cols), far_cols),
            ],
            out_specs=[
                whole(TOK, HEADS * HEAD),
                pl.BlockSpec((1, TOK, wide_cols), lambda i, tp_ref: (i, 0, 0)),
            ],
        ),
        compiler_params=params(),
        cost_estimate=pl.CostEstimate(flops=1 << 28, bytes_accessed=5 << 20, transcendentals=1 << 18),
        name="merge_project",
    )(tp_s, m0, a0, got, out_weight)
    right = [(i, (i // NX) * NX + (i + 1) % NX) for i in range(NX * NH)]
    left = [(i, (i // NX) * NX + (i + NX - 1) % NX) for i in range(NX * NH)]
    from_left = lax.ppermute(far_part[0], "tp", right)
    from_right = lax.ppermute(far_part[1], "tp", left)
    rest = pl.pallas_call(
        rest_kernel,
        out_shape=jax.ShapeDtypeStruct((6, TOK, wide_cols), BF16),
        grid_spec=pltpu.PrefetchScalarGridSpec(
            num_scalar_prefetch=1,
            grid=(6,),
            in_specs=[
                whole(TOK, HEADS * HEAD),
                pl.BlockSpec((HEADS * HEAD, wide_cols), rest_cols),
            ],
            out_specs=pl.BlockSpec((1, TOK, wide_cols), lambda i, tp_ref: (i, 0, 0)),
        ),
        compiler_params=params(),
        cost_estimate=pl.CostEstimate(flops=3 << 28, bytes_accessed=5 << 20, transcendentals=0),
        name="project_rest",
    )(tp_s, att, out_weight)
    to_right = jnp.stack([rest[0] + from_left, rest[1]])
    to_left = jnp.stack([rest[2], rest[3] + from_right])
    from_left = lax.ppermute(to_right, "tp", right)
    from_right = lax.ppermute(to_left, "tp", left)
    summed = rest[4:6].astype(F32) + from_left.astype(F32) + from_right.astype(F32)
    send = jnp.where(hi == 0, summed[1], summed[0]).astype(BF16)
    keep = jnp.where(hi == 0, summed[0], summed[1])
    swap = [(i, (i + NX) % (NX * NH)) for i in range(NX * NH)]
    projected = keep + lax.ppermute(send, "tp", swap).astype(F32)
    squares = jnp.sum(projected * projected, -1)
    squares = lax.psum(squares, "tp", axis_index_groups=[list(range(NX)), list(range(NX, 2 * NX))])
    squares = lax.psum(squares, "tp", axis_index_groups=[[i, i + NX] for i in range(NX)])
    mean_square = squares[:, None] / out_weight.shape[1]
    return (projected * lax.rsqrt(mean_square + 1e-05) * norm_gain[None, :]).astype(BF16)


def solution(mesh):
    return jax.shard_map(
        shards,
        mesh=mesh,
        in_specs=(
            P("seq", "tp"),
            P("seq", "tp"),
            P("seq", "tp"),
            P("tp"),
            P("seq", None),
            P("tp", None),
            P("tp"),
        ),
        out_specs=P("seq", "tp"),
        check_vma=False,
    )
```

```python
import functools
import math

import jax
import jax.numpy as jnp
from jax import lax
from jax.experimental import pallas as pl
from jax.experimental.pallas import tpu as pltpu
from jax.sharding import PartitionSpec as P

HEAD = 128
BLOCK = 128
LOG2E = math.log2(math.e)
NZ, NY, NC = 4, 8, 2
NX, NH = 4, 2
HEADS = 4
TOK = 256
SLOT = 2 * BLOCK
MSG = NZ * SLOT
LOW = -1e30
F32 = jnp.float32
BF16 = jnp.bfloat16

SMEM = pl.BlockSpec(memory_space=pltpu.SMEM)
VMEM = pl.BlockSpec(memory_space=pltpu.VMEM)
M_SHAPE = jax.ShapeDtypeStruct((HEADS, TOK, HEAD), F32)
ACC_SHAPE = jax.ShapeDtypeStruct((HEADS, TOK, 2 * HEAD), F32)


def sid(z, y, c):
    return (z * NY + y % NY) * NC + c


PLACES = [(z, y, c) for z in range(NZ) for y in range(NY) for c in range(NC)]
LAST = sid(NZ - 1, NY - 1, 1)


def z_perm(k):
    pairs = [(sid(z, y, c), sid(z + k, y, c)) for z, y, c in PLACES if z + k < NZ]
    return pairs + [(LAST, sid(k - 1, NY - 1, 1))]


def y_perm(k):
    return [(sid(z, y, c), sid(z, y + k, c)) for z, y, c in PLACES]


def cross(a, b):
    return lax.dot_general(a, b, (((1,), (1,)), ((), ())), preferred_element_type=F32)


def plain(a, b):
    return lax.dot_general(a, b, (((1,), (0,)), ((), ())), preferred_element_type=F32)


def wide(a, n):
    return jnp.concatenate([a] * n, axis=1)


def seen(me, query_core, key_y):
    z, y, core = me // (NY * NC), (me // NC) % NY, me % NC
    anchor = jnp.logical_and(core == 1, key_y == NY - 1)
    first_piece = (z * NY + y) * NC + query_core == 0
    below = jnp.logical_or(key_y < y, jnp.logical_and(key_y == y, core < query_core))
    own = jnp.where(anchor, jnp.logical_not(first_piece).astype(jnp.int32), below.astype(jnp.int32))
    return [own] + [(z >= k).astype(jnp.int32) for k in range(1, NZ)]


def prepare(blocks, shown, kk, vv):
    first = jnp.int32(0)
    for j in reversed(range(len(shown))):
        first = jnp.where(shown[j] > 0, j, first)
    for j, flag in enumerate(shown):
        src = jnp.where(flag > 0, j, first)
        rows = pl.multiple_of(src * SLOT, SLOT)
        kk[pl.ds(j * BLOCK, BLOCK), :] = blocks[pl.ds(rows, BLOCK), :]
        scale = flag.astype(F32)
        v = blocks[pl.ds(j * SLOT + BLOCK, BLOCK), :].astype(F32) * scale
        vv[pl.ds(j * BLOCK, BLOCK), 0:HEAD] = v.astype(BF16)
        vv[pl.ds(j * BLOCK, BLOCK), HEAD : 2 * HEAD] = jnp.full((BLOCK, HEAD), scale, F32).astype(BF16)


def update(c, q, kk, vv, m_ref, acc_ref, h):
    s = cross(q, kk[...]) * c
    m_old = m_ref[h]
    m_new = jnp.maximum(m_old, jnp.max(s, axis=1, keepdims=True))
    alpha = jnp.exp2(m_old - m_new)
    p = jnp.exp2(s - wide(m_new, s.shape[1] // HEAD)).astype(BF16)
    acc_ref[h] = acc_ref[h] * wide(alpha, 2) + plain(p, vv[...])
    m_ref[h] = m_new


def attend_set(me, core, key_ys, c, q_ref, blocks, kk, vv, m_ref, acc_ref):
    shown = []
    for key_y in key_ys:
        shown += seen(me, core, key_y)
    total = functools.reduce(lambda a, b: a + b, shown)

    @pl.when(total > 0)
    def _():
        prepare(blocks, shown, kk, vv)
        for h in range(HEADS):
            update(c, q_ref[:, h * HEAD : (h + 1) * HEAD], kk, vv, m_ref, acc_ref, h)


def first_kernel(me_ref, c_ref, q0, q1, k_ref, v_ref, blk, m0, a0, m1, a1, blocks, kk, vv, lv):
    me = me_ref[0]
    c = c_ref[0]
    core = me % NC
    lv[:, 0:HEAD] = v_ref[...]
    lv[:, HEAD : 2 * HEAD] = jnp.ones((TOK, HEAD), BF16)
    row = lax.broadcasted_iota(jnp.int32, (TOK, TOK), 0)
    col = lax.broadcasted_iota(jnp.int32, (TOK, TOK), 1)
    for h in range(HEADS):
        s = cross(q0[:, h * HEAD : (h + 1) * HEAD], k_ref[...]) * c
        s = jnp.where(row >= col, s, LOW)
        m = jnp.broadcast_to(jnp.max(s, axis=1, keepdims=True), (TOK, HEAD))
        p = jnp.exp2(s - wide(m, TOK // HEAD)).astype(BF16)
        a0[h] = plain(p, lv[...])
        m0[h] = m
        m1[h] = jnp.full((TOK, HEAD), LOW, F32)
        a1[h] = jnp.zeros((TOK, 2 * HEAD), F32)
    blocks[...] = blk[...]
    y = (me // NC) % NY
    attend_set(me, core, [y], c, q0, blocks, kk, vv, m0, a0)
    attend_set(me, 1 - core, [y], c, q1, blocks, kk, vv, m1, a1)


def ring_kernel(step, me_ref, c_ref, q0, q1, fwd, bwd, m0i, a0i, m1i, a1i, m0, a0, m1, a1, blocks, kk, vv):
    me = me_ref[0]
    c = c_ref[0]
    core = me % NC
    y = (me // NC) % NY
    m0[...] = m0i[...]
    a0[...] = a0i[...]
    m1[...] = m1i[...]
    a1[...] = a1i[...]
    blocks[0:MSG, :] = fwd[...]
    blocks[MSG : 2 * MSG, :] = bwd[...]
    key_ys = [(y + NY - step) % NY, (y + step) % NY]
    attend_set(me, core, key_ys, c, q0, blocks, kk, vv, m0, a0)
    attend_set(me, 1 - core, key_ys, c, q1, blocks, kk, vv, m1, a1)


def last_kernel(other, me_ref, c_ref, q, blk, mi, ai, *rest):
    if other:
        out, m, a, kk, vv = rest
    else:
        m, a, kk, vv = rest
    me = me_ref[0]
    core = me % NC
    y = (me // NC) % NY
    m[...] = mi[...]
    a[...] = ai[...]
    key_ys = [(y + NY // 2) % NY]
    attend_set(me, 1 - core if other else core, key_ys, c_ref[0], q, blk, kk, vv, m, a)
    if other:
        lane = lax.broadcasted_iota(jnp.int32, (TOK, HEAD), 1)
        for h in range(HEADS):
            total = a[h][:, HEAD:]
            some = total > 0.0
            safe = jnp.where(some, total, 1.0)
            out[h, :, 0:HEAD] = (a[h][:, :HEAD] / safe).astype(BF16)
            lse = jnp.where(some, m[h] + jnp.log2(safe), LOW)
            hi = lse.astype(BF16).astype(F32)
            mid = (lse - hi).astype(BF16).astype(F32)
            low = lse - hi - mid
            parts = jnp.where(lane == 0, hi, jnp.where(lane == 1, mid, low))
            out[h, :, HEAD : 2 * HEAD] = parts.astype(BF16)


def merge_kernel(tp_ref, m, a, got, w, att, out):
    @pl.when(pl.program_id(0) == 0)
    def _():
        for h in range(HEADS):
            parts = got[h][:, HEAD:].astype(F32)
            lse = (parts[:, 0:1] + parts[:, 1:2]) + parts[:, 2:3]
            mine = m[h]
            top = jnp.maximum(mine, lse)
            w0 = jnp.exp2(mine - top)
            w1 = jnp.exp2(lse - top)
            acc = a[h][:, :HEAD] * w0 + got[h][:, :HEAD].astype(F32) * w1
            total = a[h][:, HEAD:] * w0 + w1
            att[:, h * HEAD : (h + 1) * HEAD] = (acc / total).astype(BF16)

    out[0] = plain(att[...], w[...]).astype(BF16)


def rest_kernel(tp_ref, att, w, out):
    out[0] = plain(att[...], w[...]).astype(BF16)


def params(mib=20):
    return pltpu.CompilerParams(vmem_limit_bytes=mib << 20)


def scratch(n):
    return [pltpu.VMEM((n * BLOCK, HEAD), BF16), pltpu.VMEM((n * BLOCK, 2 * HEAD), BF16)]


def cost(keys, sets):
    rows = HEADS * TOK * sets
    return pl.CostEstimate(
        flops=rows * keys * HEAD * 20, bytes_accessed=4 << 20, transcendentals=rows * keys
    )


def shards(queries, keys, values, key_head_scale, retained, out_weight, norm_gain):
    me = lax.axis_index("seq").astype(jnp.int32)
    tp = lax.axis_index("tp").astype(jnp.int32)
    core, y, z = me % NC, (me // NC) % NY, me // (NC * NY)
    me_s = me.reshape(1)
    tp_s = tp.reshape(1)
    c = key_head_scale * (LOG2E / math.sqrt(HEAD))

    anchor = jnp.concatenate([keys[:BLOCK], values[:BLOCK]], 0)
    anchor_far = lax.ppermute(anchor, "seq", [(0, LAST)])
    other_queries = lax.ppermute(queries, "seq", [(sid(*s), sid(s[0], s[1], 1 - s[2])) for s in PLACES])
    row = retained[0, 0] * BLOCK
    own = jnp.concatenate(
        [
            lax.dynamic_slice_in_dim(keys, row, BLOCK, 0),
            lax.dynamic_slice_in_dim(values, row, BLOCK, 0),
        ],
        0,
    )
    own = jnp.where(me == LAST, anchor_far, own)
    up = [lax.ppermute(own, "seq", z_perm(k)) for k in range(1, NZ)]
    far = jnp.where(z == 0, up[0], jnp.where(z == 1, up[1], jnp.where(z == 2, up[2], own)))
    slot = jnp.where(jnp.logical_and(y == NY - 1, core == 1), far, own)
    block = jnp.concatenate([slot] + up, 0)

    fwd = [lax.ppermute(block, "seq", y_perm(1))]
    bwd = [lax.ppermute(block, "seq", y_perm(-1))]
    for _ in range(2):
        fwd.append(lax.ppermute(fwd[-1], "seq", y_perm(1)))
        bwd.append(lax.ppermute(bwd[-1], "seq", y_perm(-1)))
    turn = [(sid(z_, y_, c_), sid(z_, y_ + (1 if c_ == 0 else -1), c_)) for z_, y_, c_ in PLACES]
    half = lax.ppermute(jnp.where(core == 0, fwd[-1], bwd[-1]), "seq", turn)

    state_shapes = [M_SHAPE, ACC_SHAPE, M_SHAPE, ACC_SHAPE]
    state = pl.pallas_call(
        first_kernel,
        out_shape=state_shapes,
        in_specs=[SMEM, SMEM] + [VMEM] * 5,
        out_specs=[VMEM] * 4,
        scratch_shapes=[pltpu.VMEM((MSG, HEAD), BF16)] + scratch(4) + [pltpu.VMEM((TOK, 2 * HEAD), BF16)],
        compiler_params=params(),
        cost_estimate=cost(640, 2),
        name="attend_own_chip",
    )(me_s, c, queries, other_queries, keys, values, block)
    for step in range(1, 4):
        state = pl.pallas_call(
            functools.partial(ring_kernel, step),
            out_shape=state_shapes,
            in_specs=[SMEM, SMEM] + [VMEM] * 8,
            out_specs=[VMEM] * 4,
            scratch_shapes=[pltpu.VMEM((2 * MSG, HEAD), BF16)] + scratch(8),
            input_output_aliases={6: 0, 7: 1, 8: 2, 9: 3},
            compiler_params=params(),
            cost_estimate=cost(1024, 2),
            name="attend_ring",
        )(me_s, c, queries, other_queries, fwd[step - 1], bwd[step - 1], *state)
    m0, a0, m1, a1 = state
    message, _, _ = pl.pallas_call(
        functools.partial(last_kernel, True),
        out_shape=[jax.ShapeDtypeStruct((HEADS, TOK, 2 * HEAD), BF16), M_SHAPE, ACC_SHAPE],
        in_specs=[SMEM, SMEM] + [VMEM] * 4,
        out_specs=[VMEM] * 3,
        scratch_shapes=scratch(4),
        input_output_aliases={4: 1, 5: 2},
        compiler_params=params(),
        cost_estimate=cost(512, 1),
        name="attend_last_other",
    )(me_s, c, other_queries, half, m1, a1)
    got = lax.ppermute(message, "seq", [(sid(*s), sid(s[0], s[1], 1 - s[2])) for s in PLACES])
    m0, a0 = pl.pallas_call(
        functools.partial(last_kernel, False),
        out_shape=[M_SHAPE, ACC_SHAPE],
        in_specs=[SMEM, SMEM] + [VMEM] * 4,
        out_specs=[VMEM] * 2,
        scratch_shapes=scratch(4),
        input_output_aliases={4: 0, 5: 1},
        compiler_params=params(),
        cost_estimate=cost(512, 1),
        name="attend_last_own",
    )(me_s, c, queries, half, m0, a0)

    wide_cols = out_weight.shape[1] // (NX * NH)

    def column(tp_ref, own_half, d):
        tp = tp_ref[0]
        half = tp // NX if own_half else 1 - tp // NX
        return (0, half * NX + (tp + d) % NX)

    def far_cols(i, tp_ref):
        there, here = column(tp_ref, False, 2), column(tp_ref, True, 2)
        return (0, jnp.where(i == 0, there[1], here[1]))

    def rest_cols(own_half, i, tp_ref):
        return column(tp_ref, own_half, jnp.where(i == 2, 0, 1 + 2 * i))

    whole = lambda *shape: pl.BlockSpec(shape, lambda i, tp_ref: (0,) * len(shape))
    att, far_part = pl.pallas_call(
        merge_kernel,
        out_shape=[
            jax.ShapeDtypeStruct((TOK, HEADS * HEAD), BF16),
            jax.ShapeDtypeStruct((2, TOK, wide_cols), BF16),
        ],
        grid_spec=pltpu.PrefetchScalarGridSpec(
            num_scalar_prefetch=1,
            grid=(2,),
            in_specs=[
                whole(HEADS, TOK, HEAD),
                whole(HEADS, TOK, 2 * HEAD),
                whole(HEADS, TOK, 2 * HEAD),
                pl.BlockSpec((HEADS * HEAD, wide_cols), far_cols),
            ],
            out_specs=[
                whole(TOK, HEADS * HEAD),
                pl.BlockSpec((1, TOK, wide_cols), lambda i, tp_ref: (i, 0, 0)),
            ],
        ),
        compiler_params=params(),
        cost_estimate=pl.CostEstimate(flops=1 << 31, bytes_accessed=5 << 20, transcendentals=1 << 18),
        name="merge_project",
    )(tp_s, m0, a0, got, out_weight)
    right = [(i, (i // NX) * NX + (i + 1) % NX) for i in range(NX * NH)]
    left = [(i, (i // NX) * NX + (i + NX - 1) % NX) for i in range(NX * NH)]
    swap = [(i, (i + NX) % (NX * NH)) for i in range(NX * NH)]
    far_there = lax.ppermute(far_part[0], "tp", right)
    far_here = lax.ppermute(far_part[1], "tp", left)

    def rest(own_half):
        return pl.pallas_call(
            rest_kernel,
            out_shape=jax.ShapeDtypeStruct((3, TOK, wide_cols), BF16),
            grid_spec=pltpu.PrefetchScalarGridSpec(
                num_scalar_prefetch=1,
                grid=(3,),
                in_specs=[
                    whole(TOK, HEADS * HEAD),
                    pl.BlockSpec((HEADS * HEAD, wide_cols), functools.partial(rest_cols, own_half)),
                ],
                out_specs=pl.BlockSpec((1, TOK, wide_cols), lambda i, tp_ref: (i, 0, 0)),
            ),
            compiler_params=params(),
            cost_estimate=pl.CostEstimate(flops=1 << 31, bytes_accessed=2 << 20, transcendentals=0),
            name="project_rest",
        )(tp_s, att, out_weight)

    there = rest(False)
    there_left = lax.ppermute(there[0] + far_there, "tp", right)
    there_right = lax.ppermute(there[1], "tp", left)
    here = rest(True)
    here_left = lax.ppermute(here[0], "tp", right)
    here_right = lax.ppermute(here[1] + far_here, "tp", left)
    there_sum = there[2].astype(F32) + there_left.astype(F32) + there_right.astype(F32)
    crossed = lax.ppermute(there_sum.astype(BF16), "tp", swap)
    here_sum = here[2].astype(F32) + here_left.astype(F32) + here_right.astype(F32)
    projected = here_sum + crossed.astype(F32)
    squares = jnp.sum(projected * projected, -1)
    near = [[i, i + 1] for i in range(0, NX * NH, 2)]
    wrap = [[h + a, h + NX - 1 - a] for h in range(0, NX * NH, NX) for a in range(NX // 2)]
    for groups in (near, wrap):
        squares = jnp.sum(lax.all_gather(squares, "tp", axis_index_groups=groups), 0)
    squares = squares + lax.ppermute(squares, "tp", swap)
    mean_square = squares[:, None] / out_weight.shape[1]
    return (projected * lax.rsqrt(mean_square + 1e-05) * norm_gain[None, :]).astype(BF16)


def solution(mesh):
    return jax.shard_map(
        shards,
        mesh=mesh,
        in_specs=(
            P("seq", "tp"),
            P("seq", "tp"),
            P("seq", "tp"),
            P("tp"),
            P("seq", None),
            P("tp", None),
            P("tp"),
        ),
        out_specs=P("seq", "tp"),
        check_vma=False,
    )
```

```python
import functools
import math

import jax
import jax.numpy as jnp
from jax import lax
from jax.experimental import pallas as pl
from jax.experimental.pallas import tpu as pltpu
from jax.sharding import PartitionSpec as P

HEAD = 128
BLOCK = 128
LOG2E = math.log2(math.e)
NZ, NY, NC = 4, 8, 2
NX, NH = 4, 2
HEADS = 4
TOK = 256
SLOT = 2 * BLOCK
MSG = NZ * SLOT
LOW = -1e30
F32 = jnp.float32
BF16 = jnp.bfloat16

SMEM = pl.BlockSpec(memory_space=pltpu.SMEM)
VMEM = pl.BlockSpec(memory_space=pltpu.VMEM)
M_SHAPE = jax.ShapeDtypeStruct((HEADS, TOK, HEAD), F32)
ACC_SHAPE = jax.ShapeDtypeStruct((HEADS, TOK, 2 * HEAD), F32)


def sid(z, y, c):
    return (z * NY + y % NY) * NC + c


PLACES = [(z, y, c) for z in range(NZ) for y in range(NY) for c in range(NC)]


def y_perm(k):
    return [(sid(z, y, c), sid(z, y + k, c)) for z, y, c in PLACES]


def cross(a, b):
    return lax.dot_general(a, b, (((1,), (1,)), ((), ())), preferred_element_type=F32)


def plain(a, b):
    return lax.dot_general(a, b, (((1,), (0,)), ((), ())), preferred_element_type=F32)


def wide(a, n):
    return jnp.concatenate([a] * n, axis=1)


def seen(me, query_core, key_y):
    z, y, core = me // (NY * NC), (me // NC) % NY, me % NC
    holder_y = jnp.where(z == 0, 0, NY - 1)
    holder_core = jnp.where(z == 0, 0, 1)
    anchor = jnp.logical_and(core == holder_core, key_y == holder_y)
    first_piece = (z * NY + y) * NC + query_core == 0
    below = jnp.logical_or(key_y < y, jnp.logical_and(key_y == y, core < query_core)).astype(jnp.int32)
    flags = [jnp.where(j == z, below, (j < z).astype(jnp.int32)) for j in range(NZ)]
    flags[-1] = jnp.where(anchor, jnp.logical_not(first_piece).astype(jnp.int32), flags[-1])
    return flags


def prepare(blocks, shown, kk, vv):
    first = jnp.int32(0)
    for j in reversed(range(len(shown))):
        first = jnp.where(shown[j] > 0, j, first)
    for j, flag in enumerate(shown):
        src = jnp.where(flag > 0, j, first)
        rows = pl.multiple_of(src * SLOT, SLOT)
        kk[pl.ds(j * BLOCK, BLOCK), :] = blocks[pl.ds(rows, BLOCK), :]
        scale = flag.astype(F32)
        v = blocks[pl.ds(j * SLOT + BLOCK, BLOCK), :].astype(F32) * scale
        vv[pl.ds(j * BLOCK, BLOCK), 0:HEAD] = v.astype(BF16)
        vv[pl.ds(j * BLOCK, BLOCK), HEAD : 2 * HEAD] = jnp.full((BLOCK, HEAD), scale, F32).astype(BF16)


def update(c, q, kk, vv, m_ref, acc_ref, h):
    s = cross(q, kk[...]) * c
    m_old = m_ref[h]
    m_new = jnp.maximum(m_old, jnp.max(s, axis=1, keepdims=True))
    alpha = jnp.exp2(m_old - m_new)
    p = jnp.exp2(s - wide(m_new, s.shape[1] // HEAD)).astype(BF16)
    acc_ref[h] = acc_ref[h] * wide(alpha, 2) + plain(p, vv[...])
    m_ref[h] = m_new


def attend_set(me, core, key_ys, c, q_ref, blocks, kk, vv, m_ref, acc_ref):
    shown = []
    for key_y in key_ys:
        shown += seen(me, core, key_y)
    total = functools.reduce(lambda a, b: a + b, shown)

    @pl.when(total > 0)
    def _():
        prepare(blocks, shown, kk, vv)
        for h in range(HEADS):
            update(c, q_ref[:, h * HEAD : (h + 1) * HEAD], kk, vv, m_ref, acc_ref, h)


def local_kernel(c_ref, q, kv, m, a, lv):
    lv[:, 0:HEAD] = kv[:, HEAD:]
    lv[:, HEAD : 2 * HEAD] = jnp.ones((TOK, HEAD), BF16)
    c = c_ref[0]
    row = lax.broadcasted_iota(jnp.int32, (TOK, TOK), 0)
    col = lax.broadcasted_iota(jnp.int32, (TOK, TOK), 1)
    for h in range(HEADS):
        s = cross(q[:, h * HEAD : (h + 1) * HEAD], kv[:, 0:HEAD]) * c
        s = jnp.where(row >= col, s, LOW)
        top = jnp.broadcast_to(jnp.max(s, axis=1, keepdims=True), (TOK, HEAD))
        p = jnp.exp2(s - wide(top, TOK // HEAD)).astype(BF16)
        a[h] = plain(p, lv[...])
        m[h] = top


def chip_kernel(me_ref, c_ref, q0, q1, blk, m0i, a0i, m0, a0, m1, a1, kk, vv):
    me = me_ref[0]
    c = c_ref[0]
    core = me % NC
    y = (me // NC) % NY
    m0[...] = m0i[...]
    a0[...] = a0i[...]
    m1[...] = jnp.full(m1.shape, LOW, F32)
    a1[...] = jnp.zeros(a1.shape, F32)
    attend_set(me, core, [y], c, q0, blk, kk, vv, m0, a0)
    attend_set(me, 1 - core, [y], c, q1, blk, kk, vv, m1, a1)


def ring_kernel(step, me_ref, c_ref, q0, q1, fwd, bwd, m0i, a0i, m1i, a1i, m0, a0, m1, a1, blocks, kk, vv):
    me = me_ref[0]
    c = c_ref[0]
    core = me % NC
    y = (me // NC) % NY
    m0[...] = m0i[...]
    a0[...] = a0i[...]
    m1[...] = m1i[...]
    a1[...] = a1i[...]
    blocks[0:MSG, :] = fwd[...]
    blocks[MSG : 2 * MSG, :] = bwd[...]
    key_ys = [(y + NY - step) % NY, (y + step) % NY]
    attend_set(me, core, key_ys, c, q0, blocks, kk, vv, m0, a0)
    attend_set(me, 1 - core, key_ys, c, q1, blocks, kk, vv, m1, a1)


def last_kernel(other, me_ref, c_ref, q, blk, mi, ai, *rest):
    if other:
        out, m, a, kk, vv = rest
    else:
        m, a, kk, vv = rest
    me = me_ref[0]
    core = me % NC
    y = (me // NC) % NY
    m[...] = mi[...]
    a[...] = ai[...]
    key_ys = [(y + NY // 2) % NY]
    attend_set(me, 1 - core if other else core, key_ys, c_ref[0], q, blk, kk, vv, m, a)
    if other:
        lane = lax.broadcasted_iota(jnp.int32, (TOK, HEAD), 1)
        for h in range(HEADS):
            total = a[h][:, HEAD:]
            some = total > 0.0
            safe = jnp.where(some, total, 1.0)
            out[h, :, 0:HEAD] = (a[h][:, :HEAD] / safe).astype(BF16)
            lse = jnp.where(some, m[h] + jnp.log2(safe), LOW)
            hi = lse.astype(BF16).astype(F32)
            mid = (lse - hi).astype(BF16).astype(F32)
            low = lse - hi - mid
            parts = jnp.where(lane == 0, hi, jnp.where(lane == 1, mid, low))
            out[h, :, HEAD : 2 * HEAD] = parts.astype(BF16)


def merge_kernel(tp_ref, m, a, got, w, att, out):
    @pl.when(pl.program_id(0) == 0)
    def _():
        for h in range(HEADS):
            parts = got[h][:, HEAD:].astype(F32)
            lse = (parts[:, 0:1] + parts[:, 1:2]) + parts[:, 2:3]
            mine = m[h]
            top = jnp.maximum(mine, lse)
            w0 = jnp.exp2(mine - top)
            w1 = jnp.exp2(lse - top)
            acc = a[h][:, :HEAD] * w0 + got[h][:, :HEAD].astype(F32) * w1
            total = a[h][:, HEAD:] * w0 + w1
            att[:, h * HEAD : (h + 1) * HEAD] = (acc / total).astype(BF16)

    out[0] = plain(att[...], w[...]).astype(BF16)


def project_kernel(tp_ref, att, w, out):
    out[0] = plain(att[...], w[...]).astype(BF16)


def sum_kernel(parts, out):
    total = parts[0].astype(F32)
    for j in range(1, NX):
        total += parts[j].astype(F32)
    out[...] = total.astype(out.dtype)


def widen_kernel(part, out):
    out[...] = part[...].astype(F32)


def square_kernel(parts, crossed, out, squares):
    total = crossed[...]
    for j in range(NX):
        total += parts[j].astype(F32)
    out[...] = total
    ones = jnp.ones((8, total.shape[1]), F32)
    sums = lax.dot_general(
        ones,
        total * total,
        (((1,), (1,)), ((), ())),
        precision=lax.Precision.HIGHEST,
        preferred_element_type=F32,
    )
    for j in range(NX * NH):
        squares[j] = sums


def norm_kernel(features, projected, squares, gain, out):
    total = squares[0]
    for j in range(1, NX * NH):
        total += squares[j]
    scale = lax.rsqrt(jnp.transpose(total)[:, 0:1] / features + 1e-05)
    out[...] = (projected[...] * scale * gain[...]).astype(BF16)


def params(mib=20):
    return pltpu.CompilerParams(vmem_limit_bytes=mib << 20)


def scratch(n):
    return [pltpu.VMEM((n * BLOCK, HEAD), BF16), pltpu.VMEM((n * BLOCK, 2 * HEAD), BF16)]


def cost(keys, sets):
    rows = HEADS * TOK * sets
    return pl.CostEstimate(
        flops=rows * keys * HEAD * 20, bytes_accessed=4 << 20, transcendentals=rows * keys
    )


def shards(queries, keys, values, key_head_scale, retained, out_weight, norm_gain):
    me = lax.axis_index("seq").astype(jnp.int32)
    tp = lax.axis_index("tp").astype(jnp.int32)
    core, z = me % NC, me // (NC * NY)
    me_s = me.reshape(1)
    tp_s = tp.reshape(1)
    c = key_head_scale * (LOG2E / math.sqrt(HEAD))

    kv = jnp.concatenate([keys, values], 1)
    own = lax.dynamic_slice_in_dim(kv, retained[0, 0] * BLOCK, BLOCK, 0)
    own = jnp.concatenate([own[:, :HEAD], own[:, HEAD:]], 0)
    planes = [[sid(z_, y_, c_) for z_ in range(NZ)] for y_ in range(NY) for c_ in range(NC)]
    stack = lax.all_to_all(
        jnp.broadcast_to(own, (NZ, SLOT, HEAD)), "seq", 0, 0, axis_index_groups=planes
    )
    holders = [sid(z_, NY - 1, 1) for z_ in range(NZ)]
    anchor = jnp.concatenate([keys[:BLOCK], values[:BLOCK]], 0)
    far = lax.ppermute(anchor, "seq", [(0, holders[3])])
    anchor = jnp.where(me == holders[3], far, anchor)
    near = lax.ppermute(anchor, "seq", [(0, holders[1]), (holders[3], holders[2])])
    other_queries = lax.ppermute(queries, "seq", [(sid(*s), sid(s[0], s[1], 1 - s[2])) for s in PLACES])
    placed = jnp.where(jnp.logical_or(me == holders[1], me == holders[2]), near, anchor)
    holds = jnp.where(z == 0, me == 0, me % (NY * NC) == NY * NC - 1)
    block = jnp.concatenate(
        [stack[: NZ - 1].reshape(MSG - SLOT, HEAD), jnp.where(holds, placed, stack[NZ - 1])], 0
    )

    fwd = [lax.ppermute(block, "seq", y_perm(1))]
    bwd = [lax.ppermute(block, "seq", y_perm(-1))]
    for _ in range(2):
        fwd.append(lax.ppermute(fwd[-1], "seq", y_perm(1)))
        bwd.append(lax.ppermute(bwd[-1], "seq", y_perm(-1)))
    turn = [(sid(z_, y_, c_), sid(z_, y_ + (1 if c_ == 0 else -1), c_)) for z_, y_, c_ in PLACES]
    half = lax.ppermute(jnp.where(core == 0, fwd[-1], bwd[-1]), "seq", turn)

    state_shapes = [M_SHAPE, ACC_SHAPE, M_SHAPE, ACC_SHAPE]
    m0, a0 = pl.pallas_call(
        local_kernel,
        out_shape=[M_SHAPE, ACC_SHAPE],
        in_specs=[SMEM] + [VMEM] * 2,
        out_specs=[VMEM] * 2,
        scratch_shapes=[pltpu.VMEM((TOK, 2 * HEAD), BF16)],
        compiler_params=params(),
        cost_estimate=cost(512, 1),
        name="attend_local",
    )(c, queries, kv)
    state = pl.pallas_call(
        chip_kernel,
        out_shape=state_shapes,
        in_specs=[SMEM, SMEM] + [VMEM] * 5,
        out_specs=[VMEM] * 4,
        scratch_shapes=scratch(4),
        input_output_aliases={5: 0, 6: 1},
        compiler_params=params(),
        cost_estimate=cost(512, 2),
        name="attend_own_chip",
    )(me_s, c, queries, other_queries, block, m0, a0)
    for step in range(1, 4):
        state = pl.pallas_call(
            functools.partial(ring_kernel, step),
            out_shape=state_shapes,
            in_specs=[SMEM, SMEM] + [VMEM] * 8,
            out_specs=[VMEM] * 4,
            scratch_shapes=[pltpu.VMEM((2 * MSG, HEAD), BF16)] + scratch(8),
            input_output_aliases={6: 0, 7: 1, 8: 2, 9: 3},
            compiler_params=params(),
            cost_estimate=cost(1024, 2),
            name="attend_ring",
        )(me_s, c, queries, other_queries, fwd[step - 1], bwd[step - 1], *state)
    m0, a0, m1, a1 = state
    message, _, _ = pl.pallas_call(
        functools.partial(last_kernel, True),
        out_shape=[jax.ShapeDtypeStruct((HEADS, TOK, 2 * HEAD), BF16), M_SHAPE, ACC_SHAPE],
        in_specs=[SMEM, SMEM] + [VMEM] * 4,
        out_specs=[VMEM] * 3,
        scratch_shapes=scratch(4),
        input_output_aliases={4: 1, 5: 2},
        compiler_params=params(),
        cost_estimate=cost(512, 1),
        name="attend_last_other",
    )(me_s, c, other_queries, half, m1, a1)
    got = lax.ppermute(message, "seq", [(sid(*s), sid(s[0], s[1], 1 - s[2])) for s in PLACES])
    m0, a0 = pl.pallas_call(
        functools.partial(last_kernel, False),
        out_shape=[M_SHAPE, ACC_SHAPE],
        in_specs=[SMEM, SMEM] + [VMEM] * 4,
        out_specs=[VMEM] * 2,
        scratch_shapes=scratch(4),
        input_output_aliases={4: 0, 5: 1},
        compiler_params=params(),
        cost_estimate=cost(512, 1),
        name="attend_last_own",
    )(me_s, c, queries, half, m0, a0)

    wide_cols = out_weight.shape[1] // (NX * NH)

    def columns(own_half, j, tp_ref):
        half = tp_ref[0] // NX
        return (0, (half if own_half else 1 - half) * NX + j)

    whole = lambda *shape: pl.BlockSpec(shape, lambda j, tp_ref: (0,) * len(shape))
    weights = lambda own_half: pl.BlockSpec((HEADS * HEAD, wide_cols), functools.partial(columns, own_half))
    parts = pl.BlockSpec((1, TOK, wide_cols), lambda j, tp_ref: (j, 0, 0))
    parts_shape = jax.ShapeDtypeStruct((NX, TOK, wide_cols), BF16)
    att, there = pl.pallas_call(
        merge_kernel,
        out_shape=[jax.ShapeDtypeStruct((TOK, HEADS * HEAD), BF16), parts_shape],
        grid_spec=pltpu.PrefetchScalarGridSpec(
            num_scalar_prefetch=1,
            grid=(NX,),
            in_specs=[
                whole(HEADS, TOK, HEAD),
                whole(HEADS, TOK, 2 * HEAD),
                whole(HEADS, TOK, 2 * HEAD),
                weights(False),
            ],
            out_specs=[whole(TOK, HEADS * HEAD), parts],
        ),
        compiler_params=params(),
        cost_estimate=pl.CostEstimate(flops=1 << 31, bytes_accessed=5 << 20, transcendentals=1 << 18),
        name="merge_project",
    )(tp_s, m0, a0, got, out_weight)
    here = pl.pallas_call(
        project_kernel,
        out_shape=parts_shape,
        grid_spec=pltpu.PrefetchScalarGridSpec(
            num_scalar_prefetch=1,
            grid=(NX,),
            in_specs=[whole(TOK, HEADS * HEAD), weights(True)],
            out_specs=parts,
        ),
        compiler_params=params(56),
        cost_estimate=pl.CostEstimate(flops=1 << 31, bytes_accessed=2 << 20, transcendentals=0),
        name="project_own_half",
    )(tp_s, att, out_weight)
    rows = [[h * NX + x for x in range(NX)] for h in range(NH)]
    swap = [(i, (i + NX) % (NX * NH)) for i in range(NX * NH)]
    there = lax.all_to_all(there, "tp", 0, 0, axis_index_groups=rows)
    there = pl.pallas_call(
        sum_kernel,
        out_shape=jax.ShapeDtypeStruct((TOK, wide_cols), BF16),
        in_specs=[VMEM],
        out_specs=VMEM,
        compiler_params=params(),
        name="sum_other_half",
    )(there)
    crossed = pl.pallas_call(
        widen_kernel,
        out_shape=jax.ShapeDtypeStruct((TOK, wide_cols), F32),
        in_specs=[VMEM],
        out_specs=VMEM,
        compiler_params=params(),
        cost_estimate=pl.CostEstimate(flops=1 << 33, bytes_accessed=1 << 20, transcendentals=0),
        name="widen_crossed",
    )(lax.ppermute(there, "tp", swap))
    here = lax.all_to_all(here, "tp", 0, 0, axis_index_groups=rows)
    projected, squares = pl.pallas_call(
        square_kernel,
        out_shape=[
            jax.ShapeDtypeStruct((TOK, wide_cols), F32),
            jax.ShapeDtypeStruct((NX * NH, 8, TOK), F32),
        ],
        in_specs=[VMEM] * 2,
        out_specs=[VMEM] * 2,
        compiler_params=params(),
        name="sum_and_square",
    )(here, crossed)
    squares = lax.all_to_all(squares, "tp", 0, 0)
    return pl.pallas_call(
        functools.partial(norm_kernel, out_weight.shape[1]),
        out_shape=jax.ShapeDtypeStruct((TOK, wide_cols), BF16),
        in_specs=[VMEM] * 3,
        out_specs=VMEM,
        compiler_params=params(),
        name="normalize",
    )(projected, squares, norm_gain.reshape(1, wide_cols))


def solution(mesh):
    return jax.shard_map(
        shards,
        mesh=mesh,
        in_specs=(
            P("seq", "tp"),
            P("seq", "tp"),
            P("seq", "tp"),
            P("tp"),
            P("seq", None),
            P("tp", None),
            P("tp"),
        ),
        out_specs=P("seq", "tp"),
        check_vma=False,
    )
```

```python
import functools
import math

import jax
import jax.numpy as jnp
from jax import lax
from jax.experimental import pallas as pl
from jax.experimental.pallas import tpu as pltpu
from jax.sharding import PartitionSpec as P

HEAD = 128
BLOCK = 128
LOG2E = math.log2(math.e)
NZ, NY, NC = 4, 8, 2
NX, NH = 4, 2
HEADS = 4
TOK = 256
SLOT = 2 * BLOCK
MSG = NZ * SLOT
LOW = -1e30
F32 = jnp.float32
BF16 = jnp.bfloat16

SMEM = pl.BlockSpec(memory_space=pltpu.SMEM)
VMEM = pl.BlockSpec(memory_space=pltpu.VMEM)
M_SHAPE = jax.ShapeDtypeStruct((HEADS, TOK, HEAD), F32)
ACC_SHAPE = jax.ShapeDtypeStruct((HEADS, TOK, 2 * HEAD), F32)


def sid(z, y, c):
    return (z * NY + y % NY) * NC + c


PLACES = [(z, y, c) for z in range(NZ) for y in range(NY) for c in range(NC)]


def y_perm(k):
    return [(sid(z, y, c), sid(z, y + k, c)) for z, y, c in PLACES]


def cross(a, b):
    return lax.dot_general(a, b, (((1,), (1,)), ((), ())), preferred_element_type=F32)


def plain(a, b):
    return lax.dot_general(a, b, (((1,), (0,)), ((), ())), preferred_element_type=F32)


def wide(a, n):
    return jnp.concatenate([a] * n, axis=1)


def seen(me, query_core, key_y):
    z, y, core = me // (NY * NC), (me // NC) % NY, me % NC
    holder_y = jnp.where(z == 0, 0, NY - 1)
    holder_core = jnp.where(z == 0, 0, 1)
    anchor = jnp.logical_and(core == holder_core, key_y == holder_y)
    first_piece = (z * NY + y) * NC + query_core == 0
    below = jnp.logical_or(key_y < y, jnp.logical_and(key_y == y, core < query_core)).astype(jnp.int32)
    flags = [jnp.where(j == z, below, (j < z).astype(jnp.int32)) for j in range(NZ)]
    flags[-1] = jnp.where(anchor, jnp.logical_not(first_piece).astype(jnp.int32), flags[-1])
    return flags


def prepare(blocks, shown, kk, vv):
    first = jnp.int32(0)
    for j in reversed(range(len(shown))):
        first = jnp.where(shown[j] > 0, j, first)
    for j, flag in enumerate(shown):
        src = jnp.where(flag > 0, j, first)
        rows = pl.multiple_of(src * SLOT, SLOT)
        kk[pl.ds(j * BLOCK, BLOCK), :] = blocks[pl.ds(rows, BLOCK), :]
        scale = flag.astype(F32)
        v = blocks[pl.ds(j * SLOT + BLOCK, BLOCK), :].astype(F32) * scale
        vv[pl.ds(j * BLOCK, BLOCK), 0:HEAD] = v.astype(BF16)
        vv[pl.ds(j * BLOCK, BLOCK), HEAD : 2 * HEAD] = jnp.full((BLOCK, HEAD), scale, F32).astype(BF16)


def update(c, q, kk, vv, m_ref, acc_ref, h):
    s = cross(q, kk[...]) * c
    m_old = m_ref[h]
    m_new = jnp.maximum(m_old, jnp.max(s, axis=1, keepdims=True))
    alpha = jnp.exp2(m_old - m_new)
    p = jnp.exp2(s - wide(m_new, s.shape[1] // HEAD)).astype(BF16)
    acc_ref[h] = acc_ref[h] * wide(alpha, 2) + plain(p, vv[...])
    m_ref[h] = m_new


def attend_set(me, core, key_ys, c, q_ref, blocks, kk, vv, m_ref, acc_ref):
    shown = []
    for key_y in key_ys:
        shown += seen(me, core, key_y)
    total = functools.reduce(lambda a, b: a + b, shown)

    @pl.when(total > 0)
    def _():
        prepare(blocks, shown, kk, vv)
        for h in range(HEADS):
            update(c, q_ref[:, h * HEAD : (h + 1) * HEAD], kk, vv, m_ref, acc_ref, h)


def local_kernel(c_ref, q, k, v, m, a, lv):
    lv[:, 0:HEAD] = v[...]
    lv[:, HEAD : 2 * HEAD] = jnp.ones((TOK, HEAD), BF16)
    c = c_ref[0]
    row = lax.broadcasted_iota(jnp.int32, (TOK, TOK), 0)
    col = lax.broadcasted_iota(jnp.int32, (TOK, TOK), 1)
    for h in range(HEADS):
        s = cross(q[:, h * HEAD : (h + 1) * HEAD], k[...]) * c
        s = jnp.where(row >= col, s, LOW)
        top = jnp.broadcast_to(jnp.max(s, axis=1, keepdims=True), (TOK, HEAD))
        p = jnp.exp2(s - wide(top, TOK // HEAD)).astype(BF16)
        a[h] = plain(p, lv[...])
        m[h] = top


def chip_kernel(me_ref, c_ref, q0, q1, blk, m0i, a0i, m0, a0, m1, a1, kk, vv):
    me = me_ref[0]
    c = c_ref[0]
    core = me % NC
    y = (me // NC) % NY
    m0[...] = m0i[...]
    a0[...] = a0i[...]
    m1[...] = jnp.full(m1.shape, LOW, F32)
    a1[...] = jnp.zeros(a1.shape, F32)
    attend_set(me, core, [y], c, q0, blk, kk, vv, m0, a0)
    attend_set(me, 1 - core, [y], c, q1, blk, kk, vv, m1, a1)


def ring_kernel(step, me_ref, c_ref, q0, q1, fwd, bwd, m0i, a0i, m1i, a1i, m0, a0, m1, a1, blocks, kk, vv):
    me = me_ref[0]
    c = c_ref[0]
    core = me % NC
    y = (me // NC) % NY
    m0[...] = m0i[...]
    a0[...] = a0i[...]
    m1[...] = m1i[...]
    a1[...] = a1i[...]
    blocks[0:MSG, :] = fwd[...]
    blocks[MSG : 2 * MSG, :] = bwd[...]
    key_ys = [(y + NY - step) % NY, (y + step) % NY]
    attend_set(me, core, key_ys, c, q0, blocks, kk, vv, m0, a0)
    attend_set(me, 1 - core, key_ys, c, q1, blocks, kk, vv, m1, a1)


def last_kernel(other, me_ref, c_ref, q, blk, mi, ai, *rest):
    if other:
        out, m, a, kk, vv = rest
    else:
        m, a, kk, vv = rest
    me = me_ref[0]
    core = me % NC
    y = (me // NC) % NY
    m[...] = mi[...]
    a[...] = ai[...]
    key_ys = [(y + NY // 2) % NY]
    attend_set(me, 1 - core if other else core, key_ys, c_ref[0], q, blk, kk, vv, m, a)
    if other:
        lane = lax.broadcasted_iota(jnp.int32, (TOK, HEAD), 1)
        for h in range(HEADS):
            total = a[h][:, HEAD:]
            some = total > 0.0
            safe = jnp.where(some, total, 1.0)
            out[h, :, 0:HEAD] = (a[h][:, :HEAD] / safe).astype(BF16)
            lse = jnp.where(some, m[h] + jnp.log2(safe), LOW)
            hi = lse.astype(BF16).astype(F32)
            mid = (lse - hi).astype(BF16).astype(F32)
            low = lse - hi - mid
            parts = jnp.where(lane == 0, hi, jnp.where(lane == 1, mid, low))
            out[h, :, HEAD : 2 * HEAD] = parts.astype(BF16)


def merge_kernel(tp_ref, m, a, got, w, att, out):
    @pl.when(pl.program_id(0) == 0)
    def _():
        for h in range(HEADS):
            parts = got[h][:, HEAD:].astype(F32)
            lse = (parts[:, 0:1] + parts[:, 1:2]) + parts[:, 2:3]
            mine = m[h]
            top = jnp.maximum(mine, lse)
            w0 = jnp.exp2(mine - top)
            w1 = jnp.exp2(lse - top)
            acc = a[h][:, :HEAD] * w0 + got[h][:, :HEAD].astype(F32) * w1
            total = a[h][:, HEAD:] * w0 + w1
            att[:, h * HEAD : (h + 1) * HEAD] = (acc / total).astype(BF16)

    out[0] = plain(att[...], w[...]).astype(BF16)


def project_kernel(tp_ref, att, w, *outs):
    x, half = tp_ref[0] % NX, tp_ref[0] // NX
    for k, out in enumerate(outs):
        col = pl.multiple_of((half * NX + (x + k) % NX) * out.shape[1], out.shape[1])
        out[...] = plain(att[...], w[:, pl.ds(col, out.shape[1])]).astype(BF16)


def sum_kernel(parts, out):
    total = parts[0].astype(F32)
    for j in range(1, NX):
        total += parts[j].astype(F32)
    out[...] = total.astype(out.dtype)


def choose_kernel(me_ref, here, there, out):
    last = me_ref[0] == NZ * NY * NC - 1

    @pl.when(last)
    def _():
        out[...] = there[...]

    @pl.when(jnp.logical_not(last))
    def _():
        out[...] = here[...]


def square_kernel(crossed, *refs):
    *parts, out, squares = refs
    total = crossed[...].astype(F32)
    for part in parts:
        total += part[...].astype(F32)
    out[...] = total
    ones = jnp.ones((8, total.shape[1]), F32)
    sums = lax.dot_general(
        ones,
        total * total,
        (((1,), (1,)), ((), ())),
        precision=lax.Precision.HIGHEST,
        preferred_element_type=F32,
    )
    for j in range(NX * NH):
        squares[j] = sums


def norm_kernel(features, projected, squares, gain, out):
    total = squares[0]
    for j in range(1, NX * NH):
        total += squares[j]
    scale = lax.rsqrt(jnp.transpose(total)[:, 0:1] / features + 1e-05)
    out[...] = (projected[...] * scale * gain[...]).astype(BF16)


def params(mib=20):
    return pltpu.CompilerParams(vmem_limit_bytes=mib << 20)


def scratch(n):
    return [pltpu.VMEM((n * BLOCK, HEAD), BF16), pltpu.VMEM((n * BLOCK, 2 * HEAD), BF16)]


def cost(keys, sets):
    rows = HEADS * TOK * sets
    return pl.CostEstimate(
        flops=rows * keys * HEAD * 20, bytes_accessed=4 << 20, transcendentals=rows * keys
    )


def shards(queries, keys, values, key_head_scale, retained, out_weight, norm_gain):
    me = lax.axis_index("seq").astype(jnp.int32)
    tp = lax.axis_index("tp").astype(jnp.int32)
    core, z = me % NC, me // (NC * NY)
    me_s = me.reshape(1)
    tp_s = tp.reshape(1)
    c = key_head_scale * (LOG2E / math.sqrt(HEAD))

    row = retained[0, 0] * BLOCK
    own = jnp.concatenate(
        [lax.dynamic_slice_in_dim(part, row, BLOCK, 0) for part in (keys, values)], 0
    )
    planes = [[sid(z_, y_, c_) for z_ in range(NZ)] for y_ in range(NY) for c_ in range(NC)]
    stack = lax.all_to_all(
        jnp.broadcast_to(own, (NZ, SLOT, HEAD)), "seq", 0, 0, axis_index_groups=planes
    )
    holders = [sid(z_, NY - 1, 1) for z_ in range(NZ)]
    anchor = jnp.concatenate([keys[:BLOCK], values[:BLOCK]], 0)
    far = lax.ppermute(anchor, "seq", [(0, holders[3])])
    anchor = pl.pallas_call(
        choose_kernel,
        out_shape=jax.ShapeDtypeStruct((SLOT, HEAD), BF16),
        in_specs=[SMEM] + [VMEM] * 2,
        out_specs=VMEM,
        compiler_params=params(),
        cost_estimate=pl.CostEstimate(flops=1 << 33, bytes_accessed=1 << 17, transcendentals=0),
        name="choose_anchor",
    )(me_s, anchor, far)
    near = lax.ppermute(anchor, "seq", [(0, holders[1]), (holders[3], holders[2])])
    other_queries = lax.ppermute(queries, "seq", [(sid(*s), sid(s[0], s[1], 1 - s[2])) for s in PLACES])
    placed = jnp.where(jnp.logical_or(me == holders[1], me == holders[2]), near, anchor)
    holds = jnp.where(z == 0, me == 0, me % (NY * NC) == NY * NC - 1)
    block = jnp.concatenate(
        [stack[: NZ - 1].reshape(MSG - SLOT, HEAD), jnp.where(holds, placed, stack[NZ - 1])], 0
    )

    fwd = [lax.ppermute(block, "seq", y_perm(1))]
    bwd = [lax.ppermute(block, "seq", y_perm(-1))]
    for _ in range(2):
        fwd.append(lax.ppermute(fwd[-1], "seq", y_perm(1)))
        bwd.append(lax.ppermute(bwd[-1], "seq", y_perm(-1)))
    turn = [(sid(z_, y_, c_), sid(z_, y_ + (1 if c_ == 0 else -1), c_)) for z_, y_, c_ in PLACES]
    half = lax.ppermute(jnp.where(core == 0, fwd[-1], bwd[-1]), "seq", turn)

    state_shapes = [M_SHAPE, ACC_SHAPE, M_SHAPE, ACC_SHAPE]
    m0, a0 = pl.pallas_call(
        local_kernel,
        out_shape=[M_SHAPE, ACC_SHAPE],
        in_specs=[SMEM] + [VMEM] * 3,
        out_specs=[VMEM] * 2,
        scratch_shapes=[pltpu.VMEM((TOK, 2 * HEAD), BF16)],
        compiler_params=params(),
        cost_estimate=cost(512, 1),
        name="attend_local",
    )(c, queries, keys, values)
    state = pl.pallas_call(
        chip_kernel,
        out_shape=state_shapes,
        in_specs=[SMEM, SMEM] + [VMEM] * 5,
        out_specs=[VMEM] * 4,
        scratch_shapes=scratch(4),
        input_output_aliases={5: 0, 6: 1},
        compiler_params=params(),
        cost_estimate=cost(512, 2),
        name="attend_own_chip",
    )(me_s, c, queries, other_queries, block, m0, a0)
    for step in range(1, 4):
        state = pl.pallas_call(
            functools.partial(ring_kernel, step),
            out_shape=state_shapes,
            in_specs=[SMEM, SMEM] + [VMEM] * 8,
            out_specs=[VMEM] * 4,
            scratch_shapes=[pltpu.VMEM((2 * MSG, HEAD), BF16)] + scratch(8),
            input_output_aliases={6: 0, 7: 1, 8: 2, 9: 3},
            compiler_params=params(),
            cost_estimate=cost(1024, 2),
            name="attend_ring",
        )(me_s, c, queries, other_queries, fwd[step - 1], bwd[step - 1], *state)
    m0, a0, m1, a1 = state
    message, _, _ = pl.pallas_call(
        functools.partial(last_kernel, True),
        out_shape=[jax.ShapeDtypeStruct((HEADS, TOK, 2 * HEAD), BF16), M_SHAPE, ACC_SHAPE],
        in_specs=[SMEM, SMEM] + [VMEM] * 4,
        out_specs=[VMEM] * 3,
        scratch_shapes=scratch(4),
        input_output_aliases={4: 1, 5: 2},
        compiler_params=params(),
        cost_estimate=cost(512, 1),
        name="attend_last_other",
    )(me_s, c, other_queries, half, m1, a1)
    got = lax.ppermute(message, "seq", [(sid(*s), sid(s[0], s[1], 1 - s[2])) for s in PLACES])
    m0, a0 = pl.pallas_call(
        functools.partial(last_kernel, False),
        out_shape=[M_SHAPE, ACC_SHAPE],
        in_specs=[SMEM, SMEM] + [VMEM] * 4,
        out_specs=[VMEM] * 2,
        scratch_shapes=scratch(4),
        input_output_aliases={4: 0, 5: 1},
        compiler_params=params(),
        cost_estimate=cost(512, 1),
        name="attend_last_own",
    )(me_s, c, queries, half, m0, a0)

    wide_cols = out_weight.shape[1] // (NX * NH)

    def columns(own_half, j, tp_ref):
        half = tp_ref[0] // NX
        return (0, (half if own_half else 1 - half) * NX + j)

    whole = lambda *shape: pl.BlockSpec(shape, lambda j, tp_ref: (0,) * len(shape))
    weights = lambda own_half: pl.BlockSpec((HEADS * HEAD, wide_cols), functools.partial(columns, own_half))
    parts = pl.BlockSpec((1, TOK, wide_cols), lambda j, tp_ref: (j, 0, 0))
    parts_shape = jax.ShapeDtypeStruct((NX, TOK, wide_cols), BF16)
    att, there = pl.pallas_call(
        merge_kernel,
        out_shape=[jax.ShapeDtypeStruct((TOK, HEADS * HEAD), BF16), parts_shape],
        grid_spec=pltpu.PrefetchScalarGridSpec(
            num_scalar_prefetch=1,
            grid=(NX,),
            in_specs=[
                whole(HEADS, TOK, HEAD),
                whole(HEADS, TOK, 2 * HEAD),
                whole(HEADS, TOK, 2 * HEAD),
                weights(False),
            ],
            out_specs=[whole(TOK, HEADS * HEAD), parts],
        ),
        compiler_params=params(),
        cost_estimate=pl.CostEstimate(flops=1 << 31, bytes_accessed=5 << 20, transcendentals=1 << 18),
        name="merge_project",
    )(tp_s, m0, a0, got, out_weight)
    rows = [[h * NX + x for x in range(NX)] for h in range(NH)]
    swap = [(i, (i + NX) % (NX * NH)) for i in range(NX * NH)]
    there = lax.all_to_all(there, "tp", 0, 0, axis_index_groups=rows)
    here = pl.pallas_call(
        project_kernel,
        out_shape=[jax.ShapeDtypeStruct((TOK, wide_cols), BF16)] * NX,
        in_specs=[SMEM] + [VMEM] * 2,
        out_specs=[VMEM] * NX,
        compiler_params=params(),
        cost_estimate=pl.CostEstimate(flops=1 << 31, bytes_accessed=2 << 20, transcendentals=0),
        name="project_own_half",
    )(tp_s, att, out_weight)
    here = [here[0]] + [
        lax.ppermute(here[k], "tp", [(i, i // NX * NX + (i + k) % NX) for i in range(NX * NH)])
        for k in range(1, NX)
    ]
    there = pl.pallas_call(
        sum_kernel,
        out_shape=jax.ShapeDtypeStruct((TOK, wide_cols), BF16),
        in_specs=[VMEM],
        out_specs=VMEM,
        compiler_params=params(),
        name="sum_other_half",
    )(there)
    crossed = lax.ppermute(there, "tp", swap)
    projected, squares = pl.pallas_call(
        square_kernel,
        out_shape=[
            jax.ShapeDtypeStruct((TOK, wide_cols), F32),
            jax.ShapeDtypeStruct((NX * NH, 8, TOK), F32),
        ],
        in_specs=[VMEM] * (NX + 1),
        out_specs=[VMEM] * 2,
        compiler_params=params(),
        name="sum_and_square",
    )(crossed, *here)
    squares = lax.all_to_all(squares, "tp", 0, 0)
    return pl.pallas_call(
        functools.partial(norm_kernel, out_weight.shape[1]),
        out_shape=jax.ShapeDtypeStruct((TOK, wide_cols), BF16),
        in_specs=[VMEM] * 3,
        out_specs=VMEM,
        compiler_params=params(),
        name="normalize",
    )(projected, squares, norm_gain.reshape(1, wide_cols))


def solution(mesh):
    return jax.shard_map(
        shards,
        mesh=mesh,
        in_specs=(
            P("seq", "tp"),
            P("seq", "tp"),
            P("seq", "tp"),
            P("tp"),
            P("seq", None),
            P("tp", None),
            P("tp"),
        ),
        out_specs=P("seq", "tp"),
        check_vma=False,
    )
```

```python
import functools
import math

import jax
import jax.numpy as jnp
from jax import lax
from jax.experimental import pallas as pl
from jax.experimental.pallas import tpu as pltpu
from jax.sharding import PartitionSpec as P

HEAD = 128
BLOCK = 128
LOG2E = math.log2(math.e)
NZ, NY, NC = 4, 8, 2
NX, NH = 4, 2
HEADS = 4
TOK = 256
SLOT = 2 * BLOCK
MSG = NZ * SLOT
LOW = -1e30
F32 = jnp.float32
BF16 = jnp.bfloat16

SMEM = pl.BlockSpec(memory_space=pltpu.SMEM)
VMEM = pl.BlockSpec(memory_space=pltpu.VMEM)
M_SHAPE = jax.ShapeDtypeStruct((HEADS, TOK, HEAD), F32)
ACC_SHAPE = jax.ShapeDtypeStruct((HEADS, TOK, 2 * HEAD), F32)


def sid(z, y, c):
    return (z * NY + y % NY) * NC + c


PLACES = [(z, y, c) for z in range(NZ) for y in range(NY) for c in range(NC)]


def y_perm(k):
    return [(sid(z, y, c), sid(z, y + k, c)) for z, y, c in PLACES]


def cross(a, b):
    return lax.dot_general(a, b, (((1,), (1,)), ((), ())), preferred_element_type=F32)


def plain(a, b):
    return lax.dot_general(a, b, (((1,), (0,)), ((), ())), preferred_element_type=F32)


def wide(a, n):
    return jnp.concatenate([a] * n, axis=1)


def seen(me, query_core, key_y):
    z, y, core = me // (NY * NC), (me // NC) % NY, me % NC
    holder_y = jnp.where(z == 0, 0, NY - 1)
    holder_core = jnp.where(z == 0, 0, 1)
    anchor = jnp.logical_and(core == holder_core, key_y == holder_y)
    first_piece = (z * NY + y) * NC + query_core == 0
    below = jnp.logical_or(key_y < y, jnp.logical_and(key_y == y, core < query_core)).astype(jnp.int32)
    flags = [jnp.where(j == z, below, (j < z).astype(jnp.int32)) for j in range(NZ)]
    flags[-1] = jnp.where(anchor, jnp.logical_not(first_piece).astype(jnp.int32), flags[-1])
    return flags


def prepare(blocks, shown, kk, vv):
    first = jnp.int32(0)
    for j in reversed(range(len(shown))):
        first = jnp.where(shown[j] > 0, j, first)
    for j, flag in enumerate(shown):
        src = jnp.where(flag > 0, j, first)
        rows = pl.multiple_of(src * SLOT, SLOT)
        kk[pl.ds(j * BLOCK, BLOCK), :] = blocks[pl.ds(rows, BLOCK), :]
        scale = flag.astype(F32)
        v = blocks[pl.ds(j * SLOT + BLOCK, BLOCK), :].astype(F32) * scale
        vv[pl.ds(j * BLOCK, BLOCK), 0:HEAD] = v.astype(BF16)
        vv[pl.ds(j * BLOCK, BLOCK), HEAD : 2 * HEAD] = jnp.full((BLOCK, HEAD), scale, F32).astype(BF16)


def update(c, q, kk, vv, old, new, h):
    s = cross(q, kk[...]) * c
    m_old = old[0][h]
    m_new = jnp.maximum(m_old, jnp.max(s, axis=1, keepdims=True))
    alpha = jnp.exp2(m_old - m_new)
    p = jnp.exp2(s - wide(m_new, s.shape[1] // HEAD)).astype(BF16)
    new[1][h] = old[1][h] * wide(alpha, 2) + plain(p, vv[...])
    new[0][h] = m_new


def attend_set(me, core, key_ys, c, q_ref, blocks, kk, vv, old, new):
    shown = []
    for key_y in key_ys:
        shown += seen(me, core, key_y)
    total = functools.reduce(lambda a, b: a + b, shown)

    @pl.when(total > 0)
    def _():
        prepare(blocks, shown, kk, vv)
        for h in range(HEADS):
            update(c, q_ref[:, h * HEAD : (h + 1) * HEAD], kk, vv, old, new, h)

    if old is not new:

        @pl.when(total == 0)
        def _():
            for source, target in zip(old, new):
                target[...] = source[...]


def local_kernel(c_ref, q, k, v, m, a, lv):
    lv[:, 0:HEAD] = v[...]
    lv[:, HEAD : 2 * HEAD] = jnp.ones((TOK, HEAD), BF16)
    c = c_ref[0]
    row = lax.broadcasted_iota(jnp.int32, (TOK, TOK), 0)
    col = lax.broadcasted_iota(jnp.int32, (TOK, TOK), 1)
    for h in range(HEADS):
        s = cross(q[:, h * HEAD : (h + 1) * HEAD], k[...]) * c
        s = jnp.where(row >= col, s, LOW)
        top = jnp.broadcast_to(jnp.max(s, axis=1, keepdims=True), (TOK, HEAD))
        p = jnp.exp2(s - wide(top, TOK // HEAD)).astype(BF16)
        a[h] = plain(p, lv[...])
        m[h] = top


def chip_kernel(me_ref, c_ref, q0, q1, blk, m0i, a0i, m0, a0, m1, a1, kk, vv):
    me = me_ref[0]
    c = c_ref[0]
    core = me % NC
    y = (me // NC) % NY
    m1[...] = jnp.full(m1.shape, LOW, F32)
    a1[...] = jnp.zeros(a1.shape, F32)
    attend_set(me, core, [y], c, q0, blk, kk, vv, (m0i, a0i), (m0, a0))
    start = (m1, a1)
    attend_set(me, 1 - core, [y], c, q1, blk, kk, vv, start, start)


def ring_kernel(step, me_ref, c_ref, q0, q1, fwd, bwd, m0i, a0i, m1i, a1i, m0, a0, m1, a1, blocks, kk, vv):
    me = me_ref[0]
    c = c_ref[0]
    core = me % NC
    y = (me // NC) % NY
    blocks[0:MSG, :] = fwd[...]
    blocks[MSG : 2 * MSG, :] = bwd[...]
    key_ys = [(y + NY - step) % NY, (y + step) % NY]
    attend_set(me, core, key_ys, c, q0, blocks, kk, vv, (m0i, a0i), (m0, a0))
    attend_set(me, 1 - core, key_ys, c, q1, blocks, kk, vv, (m1i, a1i), (m1, a1))


def last_kernel(other, me_ref, c_ref, q, blk, mi, ai, *rest):
    if other:
        out, m, a, kk, vv = rest
    else:
        m, a, kk, vv = rest
    me = me_ref[0]
    core = me % NC
    y = (me // NC) % NY
    key_ys = [(y + NY // 2) % NY]
    attend_set(me, 1 - core if other else core, key_ys, c_ref[0], q, blk, kk, vv, (mi, ai), (m, a))
    if other:
        lane = lax.broadcasted_iota(jnp.int32, (TOK, HEAD), 1)
        for h in range(HEADS):
            total = a[h][:, HEAD:]
            some = total > 0.0
            safe = jnp.where(some, total, 1.0)
            out[h, :, 0:HEAD] = (a[h][:, :HEAD] / safe).astype(BF16)
            lse = jnp.where(some, m[h] + jnp.log2(safe), LOW)
            hi = lse.astype(BF16).astype(F32)
            mid = (lse - hi).astype(BF16).astype(F32)
            low = lse - hi - mid
            parts = jnp.where(lane == 0, hi, jnp.where(lane == 1, mid, low))
            out[h, :, HEAD : 2 * HEAD] = parts.astype(BF16)


def merge_kernel(tp_ref, m, a, got, w, there, *rest):
    *here, att = rest
    for h in range(HEADS):
        parts = got[h][:, HEAD:].astype(F32)
        lse = (parts[:, 0:1] + parts[:, 1:2]) + parts[:, 2:3]
        mine = m[h]
        top = jnp.maximum(mine, lse)
        w0 = jnp.exp2(mine - top)
        w1 = jnp.exp2(lse - top)
        acc = a[h][:, :HEAD] * w0 + got[h][:, :HEAD].astype(F32) * w1
        total = a[h][:, HEAD:] * w0 + w1
        att[:, h * HEAD : (h + 1) * HEAD] = (acc / total).astype(BF16)
    x, half = tp_ref[0] % NX, tp_ref[0] // NX
    cols = there.shape[2]

    def project(half, j):
        return plain(att[...], w[:, pl.ds(pl.multiple_of((half * NX + j) * cols, cols), cols)]).astype(BF16)

    for j in range(NX):
        there[j] = project(1 - half, j)
    for k in range(NX):
        here[k][...] = project(half, (x + k) % NX)


def sum_kernel(parts, part, out, same):
    total = parts[0].astype(F32)
    for j in range(1, NX):
        total += parts[j].astype(F32)
    out[...] = total.astype(BF16)
    same[...] = part[...]


def add_kernel(*refs):
    *parts, out = refs
    total = parts[0][...].astype(F32)
    for part in parts[1:]:
        total += part[...].astype(F32)
    out[...] = total


def choose_kernel(me_ref, here, there, out):
    last = me_ref[0] == NZ * NY * NC - 1

    @pl.when(last)
    def _():
        out[...] = there[...]

    @pl.when(jnp.logical_not(last))
    def _():
        out[...] = here[...]


def square_kernel(part, last, out, squares):
    total = part[...] + last[...].astype(F32)
    out[...] = total
    ones = jnp.ones((8, total.shape[1]), F32)
    sums = lax.dot_general(
        ones,
        total * total,
        (((1,), (1,)), ((), ())),
        precision=lax.Precision.HIGHEST,
        preferred_element_type=F32,
    )
    for j in range(NX * NH):
        squares[j] = sums


def norm_kernel(features, projected, squares, gain, out):
    total = squares[0]
    for j in range(1, NX * NH):
        total += squares[j]
    scale = lax.rsqrt(jnp.transpose(total)[:, 0:1] / features + 1e-05)
    out[...] = (projected[...] * scale * gain[...]).astype(BF16)


def params(mib=20):
    return pltpu.CompilerParams(vmem_limit_bytes=mib << 20)


def scratch(n):
    return [pltpu.VMEM((n * BLOCK, HEAD), BF16), pltpu.VMEM((n * BLOCK, 2 * HEAD), BF16)]


def cost(keys, sets):
    rows = HEADS * TOK * sets
    return pl.CostEstimate(
        flops=rows * keys * HEAD * 20, bytes_accessed=4 << 20, transcendentals=rows * keys
    )


def shards(queries, keys, values, key_head_scale, retained, out_weight, norm_gain):
    me = lax.axis_index("seq").astype(jnp.int32)
    tp = lax.axis_index("tp").astype(jnp.int32)
    core, z = me % NC, me // (NC * NY)
    me_s = me.reshape(1)
    tp_s = tp.reshape(1)
    c = key_head_scale * (LOG2E / math.sqrt(HEAD))

    row = retained[0, 0] * BLOCK
    own = jnp.concatenate(
        [lax.dynamic_slice_in_dim(part, row, BLOCK, 0) for part in (keys, values)], 0
    )
    planes = [[sid(z_, y_, c_) for z_ in range(NZ)] for y_ in range(NY) for c_ in range(NC)]
    stack = lax.all_to_all(
        jnp.broadcast_to(own, (NZ, SLOT, HEAD)), "seq", 0, 0, axis_index_groups=planes
    )
    holders = [sid(z_, NY - 1, 1) for z_ in range(NZ)]
    anchor = jnp.concatenate([keys[:BLOCK], values[:BLOCK]], 0)
    far = lax.ppermute(anchor, "seq", [(0, holders[3])])
    anchor = pl.pallas_call(
        choose_kernel,
        out_shape=jax.ShapeDtypeStruct((SLOT, HEAD), BF16),
        in_specs=[SMEM] + [VMEM] * 2,
        out_specs=VMEM,
        compiler_params=params(),
        cost_estimate=pl.CostEstimate(flops=1 << 33, bytes_accessed=1 << 17, transcendentals=0),
        name="choose_anchor",
    )(me_s, anchor, far)
    near = lax.ppermute(anchor, "seq", [(0, holders[1]), (holders[3], holders[2])])
    other_queries = lax.ppermute(queries, "seq", [(sid(*s), sid(s[0], s[1], 1 - s[2])) for s in PLACES])
    placed = jnp.where(jnp.logical_or(me == holders[1], me == holders[2]), near, anchor)
    holds = jnp.where(z == 0, me == 0, me % (NY * NC) == NY * NC - 1)
    block = jnp.concatenate(
        [stack[: NZ - 1].reshape(MSG - SLOT, HEAD), jnp.where(holds, placed, stack[NZ - 1])], 0
    )

    fwd = [lax.ppermute(block, "seq", y_perm(1))]
    bwd = [lax.ppermute(block, "seq", y_perm(-1))]
    for _ in range(2):
        fwd.append(lax.ppermute(fwd[-1], "seq", y_perm(1)))
        bwd.append(lax.ppermute(bwd[-1], "seq", y_perm(-1)))
    turn = [(sid(z_, y_, c_), sid(z_, y_ + (1 if c_ == 0 else -1), c_)) for z_, y_, c_ in PLACES]
    half = lax.ppermute(jnp.where(core == 0, fwd[-1], bwd[-1]), "seq", turn)

    state_shapes = [M_SHAPE, ACC_SHAPE, M_SHAPE, ACC_SHAPE]
    m0, a0 = pl.pallas_call(
        local_kernel,
        out_shape=[M_SHAPE, ACC_SHAPE],
        in_specs=[SMEM] + [VMEM] * 3,
        out_specs=[VMEM] * 2,
        scratch_shapes=[pltpu.VMEM((TOK, 2 * HEAD), BF16)],
        compiler_params=params(),
        cost_estimate=cost(512, 1),
        name="attend_local",
    )(c, queries, keys, values)
    state = pl.pallas_call(
        chip_kernel,
        out_shape=state_shapes,
        in_specs=[SMEM, SMEM] + [VMEM] * 5,
        out_specs=[VMEM] * 4,
        scratch_shapes=scratch(4),
        input_output_aliases={5: 0, 6: 1},
        compiler_params=params(),
        cost_estimate=cost(512, 2),
        name="attend_own_chip",
    )(me_s, c, queries, other_queries, block, m0, a0)
    for step in range(1, 4):
        state = pl.pallas_call(
            functools.partial(ring_kernel, step),
            out_shape=state_shapes,
            in_specs=[SMEM, SMEM] + [VMEM] * 8,
            out_specs=[VMEM] * 4,
            scratch_shapes=[pltpu.VMEM((2 * MSG, HEAD), BF16)] + scratch(8),
            input_output_aliases={6: 0, 7: 1, 8: 2, 9: 3},
            compiler_params=params(),
            cost_estimate=cost(1024, 2),
            name="attend_ring",
        )(me_s, c, queries, other_queries, fwd[step - 1], bwd[step - 1], *state)
    m0, a0, m1, a1 = state
    message, _, _ = pl.pallas_call(
        functools.partial(last_kernel, True),
        out_shape=[jax.ShapeDtypeStruct((HEADS, TOK, 2 * HEAD), BF16), M_SHAPE, ACC_SHAPE],
        in_specs=[SMEM, SMEM] + [VMEM] * 4,
        out_specs=[VMEM] * 3,
        scratch_shapes=scratch(4),
        input_output_aliases={4: 1, 5: 2},
        compiler_params=params(),
        cost_estimate=cost(512, 1),
        name="attend_last_other",
    )(me_s, c, other_queries, half, m1, a1)
    got = lax.ppermute(message, "seq", [(sid(*s), sid(s[0], s[1], 1 - s[2])) for s in PLACES])
    m0, a0 = pl.pallas_call(
        functools.partial(last_kernel, False),
        out_shape=[M_SHAPE, ACC_SHAPE],
        in_specs=[SMEM, SMEM] + [VMEM] * 4,
        out_specs=[VMEM] * 2,
        scratch_shapes=scratch(4),
        input_output_aliases={4: 0, 5: 1},
        compiler_params=params(),
        cost_estimate=cost(512, 1),
        name="attend_last_own",
    )(me_s, c, queries, half, m0, a0)

    wide_cols = out_weight.shape[1] // (NX * NH)

    block_shape = jax.ShapeDtypeStruct((TOK, wide_cols), BF16)
    there, *here = pl.pallas_call(
        merge_kernel,
        out_shape=[jax.ShapeDtypeStruct((NX, TOK, wide_cols), BF16)] + [block_shape] * NX,
        in_specs=[SMEM] + [VMEM] * 4,
        out_specs=[VMEM] * (NX + 1),
        scratch_shapes=[pltpu.VMEM((TOK, HEADS * HEAD), BF16)],
        compiler_params=params(),
        cost_estimate=pl.CostEstimate(flops=1 << 32, bytes_accessed=8 << 20, transcendentals=1 << 18),
        name="merge_project",
    )(tp_s, m0, a0, got, out_weight)
    rows = [[h * NX + x for x in range(NX)] for h in range(NH)]
    swap = [(i, (i + NX) % (NX * NH)) for i in range(NX * NH)]

    def turn_x(part, k):
        return lax.ppermute(part, "tp", [(i, i // NX * NX + (i + k) % NX) for i in range(NX * NH)])

    there = lax.all_to_all(there, "tp", 0, 0, axis_index_groups=rows)
    second, first = turn_x(here[2], 2), turn_x(here[1], 1)
    there, third = pl.pallas_call(
        sum_kernel,
        out_shape=[block_shape] * 2,
        in_specs=[VMEM] * 2,
        out_specs=[VMEM] * 2,
        compiler_params=params(),
        name="sum_other_half",
    )(there, here[3])

    def add(flops, *parts):
        return pl.pallas_call(
            add_kernel,
            out_shape=jax.ShapeDtypeStruct((TOK, wide_cols), F32),
            in_specs=[VMEM] * len(parts),
            out_specs=VMEM,
            compiler_params=params(),
            cost_estimate=pl.CostEstimate(flops=flops, bytes_accessed=1 << 20, transcendentals=0),
            name="add_parts",
        )(*parts)

    third = turn_x(third, 3)
    part = add(1 << 31, here[0], first, second)
    part = add(1 << 30, part, lax.ppermute(there, "tp", swap))
    projected, squares = pl.pallas_call(
        square_kernel,
        out_shape=[
            jax.ShapeDtypeStruct((TOK, wide_cols), F32),
            jax.ShapeDtypeStruct((NX * NH, 8, TOK), F32),
        ],
        in_specs=[VMEM] * 2,
        out_specs=[VMEM] * 2,
        compiler_params=params(),
        name="sum_and_square",
    )(part, third)
    squares = lax.all_to_all(squares, "tp", 0, 0)
    return pl.pallas_call(
        functools.partial(norm_kernel, out_weight.shape[1]),
        out_shape=jax.ShapeDtypeStruct((TOK, wide_cols), BF16),
        in_specs=[VMEM] * 3,
        out_specs=VMEM,
        compiler_params=params(),
        name="normalize",
    )(projected, squares, norm_gain.reshape(1, wide_cols))


def solution(mesh):
    return jax.shard_map(
        shards,
        mesh=mesh,
        in_specs=(
            P("seq", "tp"),
            P("seq", "tp"),
            P("seq", "tp"),
            P("tp"),
            P("seq", None),
            P("tp", None),
            P("tp"),
        ),
        out_specs=P("seq", "tp"),
        check_vma=False,
    )
```

```python
import functools
import math

import jax
import jax.numpy as jnp
from jax import lax
from jax.experimental import pallas as pl
from jax.experimental.pallas import tpu as pltpu
from jax.sharding import PartitionSpec as P

HEAD = 128
BLOCK = 128
LOG2E = math.log2(math.e)
NZ, NY, NC = 4, 8, 2
NX, NH = 4, 2
HEADS = 4
TOK = 256
SLOT = 2 * BLOCK
MSG = NZ * SLOT
LOW = -1e30
F32 = jnp.float32
BF16 = jnp.bfloat16

SMEM = pl.BlockSpec(memory_space=pltpu.SMEM)
VMEM = pl.BlockSpec(memory_space=pltpu.VMEM)
M_SHAPE = jax.ShapeDtypeStruct((HEADS, TOK, HEAD), F32)
ACC_SHAPE = jax.ShapeDtypeStruct((HEADS, TOK, 2 * HEAD), F32)


def sid(z, y, c):
    return (z * NY + y % NY) * NC + c


PLACES = [(z, y, c) for z in range(NZ) for y in range(NY) for c in range(NC)]


def y_perm(k):
    return [(sid(z, y, c), sid(z, y + k, c)) for z, y, c in PLACES]


def cross(a, b):
    return lax.dot_general(a, b, (((1,), (1,)), ((), ())), preferred_element_type=F32)


def plain(a, b):
    return lax.dot_general(a, b, (((1,), (0,)), ((), ())), preferred_element_type=F32)


def wide(a, n):
    return jnp.concatenate([a] * n, axis=1)


def seen(me, query_core, key_y):
    z, y, core = me // (NY * NC), (me // NC) % NY, me % NC
    holder_y = jnp.where(z == 0, 0, NY - 1)
    holder_core = jnp.where(z == 0, 0, 1)
    anchor = jnp.logical_and(core == holder_core, key_y == holder_y)
    first_piece = (z * NY + y) * NC + query_core == 0
    below = jnp.logical_or(key_y < y, jnp.logical_and(key_y == y, core < query_core)).astype(jnp.int32)
    flags = [jnp.where(j == z, below, (j < z).astype(jnp.int32)) for j in range(NZ)]
    flags[-1] = jnp.where(anchor, jnp.logical_not(first_piece).astype(jnp.int32), flags[-1])
    return flags


def prepare(blocks, shown, kk, vv):
    first = jnp.int32(0)
    for j in reversed(range(len(shown))):
        first = jnp.where(shown[j] > 0, j, first)
    for j, flag in enumerate(shown):
        src = jnp.where(flag > 0, j, first)
        rows = pl.multiple_of(src * SLOT, SLOT)
        kk[pl.ds(j * BLOCK, BLOCK), :] = blocks[pl.ds(rows, BLOCK), :]
        scale = flag.astype(F32)
        v = blocks[pl.ds(j * SLOT + BLOCK, BLOCK), :].astype(F32) * scale
        vv[pl.ds(j * BLOCK, BLOCK), 0:HEAD] = v.astype(BF16)
        vv[pl.ds(j * BLOCK, BLOCK), HEAD : 2 * HEAD] = jnp.full((BLOCK, HEAD), scale, F32).astype(BF16)


def update(c, q, kk, vv, m_ref, acc_ref, h):
    s = cross(q, kk[...]) * c
    m_old = m_ref[h]
    m_new = jnp.maximum(m_old, jnp.max(s, axis=1, keepdims=True))
    alpha = jnp.exp2(m_old - m_new)
    p = jnp.exp2(s - wide(m_new, s.shape[1] // HEAD)).astype(BF16)
    acc_ref[h] = acc_ref[h] * wide(alpha, 2) + plain(p, vv[...])
    m_ref[h] = m_new


def attend_set(me, core, key_ys, c, q_ref, blocks, kk, vv, m_ref, acc_ref):
    shown = []
    for key_y in key_ys:
        shown += seen(me, core, key_y)
    total = functools.reduce(lambda a, b: a + b, shown)

    @pl.when(total > 0)
    def _():
        prepare(blocks, shown, kk, vv)
        for h in range(HEADS):
            update(c, q_ref[:, h * HEAD : (h + 1) * HEAD], kk, vv, m_ref, acc_ref, h)


def local_kernel(c_ref, q, k, v, m, a, lv):
    lv[:, 0:HEAD] = v[...]
    lv[:, HEAD : 2 * HEAD] = jnp.ones((TOK, HEAD), BF16)
    c = c_ref[0]
    row = lax.broadcasted_iota(jnp.int32, (TOK, TOK), 0)
    col = lax.broadcasted_iota(jnp.int32, (TOK, TOK), 1)
    for h in range(HEADS):
        s = cross(q[:, h * HEAD : (h + 1) * HEAD], k[...]) * c
        s = jnp.where(row >= col, s, LOW)
        top = jnp.broadcast_to(jnp.max(s, axis=1, keepdims=True), (TOK, HEAD))
        p = jnp.exp2(s - wide(top, TOK // HEAD)).astype(BF16)
        a[h] = plain(p, lv[...])
        m[h] = top


def chip_kernel(me_ref, c_ref, q0, q1, blk, m0i, a0i, m0, a0, m1, a1, kk, vv):
    me = me_ref[0]
    c = c_ref[0]
    core = me % NC
    y = (me // NC) % NY
    m0[...] = m0i[...]
    a0[...] = a0i[...]
    m1[...] = jnp.full(m1.shape, LOW, F32)
    a1[...] = jnp.zeros(a1.shape, F32)
    attend_set(me, core, [y], c, q0, blk, kk, vv, m0, a0)
    attend_set(me, 1 - core, [y], c, q1, blk, kk, vv, m1, a1)


def ring_kernel(step, me_ref, c_ref, q0, q1, fwd, bwd, m0i, a0i, m1i, a1i, m0, a0, m1, a1, blocks, kk, vv):
    me = me_ref[0]
    c = c_ref[0]
    core = me % NC
    y = (me // NC) % NY
    m0[...] = m0i[...]
    a0[...] = a0i[...]
    m1[...] = m1i[...]
    a1[...] = a1i[...]
    blocks[0:MSG, :] = fwd[...]
    blocks[MSG : 2 * MSG, :] = bwd[...]
    key_ys = [(y + NY - step) % NY, (y + step) % NY]
    attend_set(me, core, key_ys, c, q0, blocks, kk, vv, m0, a0)
    attend_set(me, 1 - core, key_ys, c, q1, blocks, kk, vv, m1, a1)


def last_kernel(other, me_ref, c_ref, q, blk, mi, ai, *rest):
    if other:
        out, m, a, kk, vv = rest
    else:
        m, a, kk, vv = rest
    me = me_ref[0]
    core = me % NC
    y = (me // NC) % NY
    m[...] = mi[...]
    a[...] = ai[...]
    key_ys = [(y + NY // 2) % NY]
    attend_set(me, 1 - core if other else core, key_ys, c_ref[0], q, blk, kk, vv, m, a)
    if other:
        lane = lax.broadcasted_iota(jnp.int32, (TOK, HEAD), 1)
        for h in range(HEADS):
            total = a[h][:, HEAD:]
            some = total > 0.0
            safe = jnp.where(some, total, 1.0)
            out[h, :, 0:HEAD] = (a[h][:, :HEAD] / safe).astype(BF16)
            lse = jnp.where(some, m[h] + jnp.log2(safe), LOW)
            hi = lse.astype(BF16).astype(F32)
            mid = (lse - hi).astype(BF16).astype(F32)
            low = lse - hi - mid
            parts = jnp.where(lane == 0, hi, jnp.where(lane == 1, mid, low))
            out[h, :, HEAD : 2 * HEAD] = parts.astype(BF16)


def project(att, w, half, j, cols):
    return plain(att[...], w[:, pl.ds(pl.multiple_of((half * NX + j) * cols, cols), cols)]).astype(BF16)


def merge_kernel(tp_ref, m, a, got, w, att, there):
    for h in range(HEADS):
        parts = got[h][:, HEAD:].astype(F32)
        lse = (parts[:, 0:1] + parts[:, 1:2]) + parts[:, 2:3]
        mine = m[h]
        top = jnp.maximum(mine, lse)
        w0 = jnp.exp2(mine - top)
        w1 = jnp.exp2(lse - top)
        acc = a[h][:, :HEAD] * w0 + got[h][:, :HEAD].astype(F32) * w1
        total = a[h][:, HEAD:] * w0 + w1
        att[:, h * HEAD : (h + 1) * HEAD] = (acc / total).astype(BF16)
    for j in range(NX):
        there[j] = project(att, w, 1 - tp_ref[0] // NX, j, there.shape[2])


def own_kernel(tp_ref, att, w, *outs):
    x, half = tp_ref[0] % NX, tp_ref[0] // NX
    for k, out in enumerate(outs):
        out[...] = project(att, w, half, (x + k) % NX, out.shape[1])


def sum_kernel(parts, *refs):
    total = parts[0].astype(F32)
    for j in range(1, NX):
        total += parts[j].astype(F32)
    out, *same = refs[NX - 1 :]
    out[...] = total.astype(BF16)
    for source, target in zip(refs, same):
        target[...] = source[...]


def add_kernel(*refs):
    *parts, out = refs
    total = parts[0][...].astype(F32)
    for part in parts[1:]:
        total += part[...].astype(F32)
    out[...] = total


def choose_kernel(me_ref, here, there, out):
    last = me_ref[0] == NZ * NY * NC - 1

    @pl.when(last)
    def _():
        out[...] = there[...]

    @pl.when(jnp.logical_not(last))
    def _():
        out[...] = here[...]


def square_kernel(part, *refs):
    *parts, out, squares = refs
    total = part[...]
    for other in parts:
        total += other[...].astype(F32)
    out[...] = total
    ones = jnp.ones((8, total.shape[1]), F32)
    sums = lax.dot_general(
        ones,
        total * total,
        (((1,), (1,)), ((), ())),
        precision=lax.Precision.HIGHEST,
        preferred_element_type=F32,
    )
    for j in range(NX * NH):
        squares[j] = sums


def norm_kernel(features, projected, squares, gain, out):
    total = squares[0]
    for j in range(1, NX * NH):
        total += squares[j]
    scale = lax.rsqrt(jnp.transpose(total)[:, 0:1] / features + 1e-05)
    out[...] = (projected[...] * scale * gain[...]).astype(BF16)


def params(mib=20):
    return pltpu.CompilerParams(vmem_limit_bytes=mib << 20)


def scratch(n):
    return [pltpu.VMEM((n * BLOCK, HEAD), BF16), pltpu.VMEM((n * BLOCK, 2 * HEAD), BF16)]


def cost(keys, sets):
    rows = HEADS * TOK * sets
    return pl.CostEstimate(
        flops=rows * keys * HEAD * 20, bytes_accessed=4 << 20, transcendentals=rows * keys
    )


def shards(queries, keys, values, key_head_scale, retained, out_weight, norm_gain):
    me = lax.axis_index("seq").astype(jnp.int32)
    tp = lax.axis_index("tp").astype(jnp.int32)
    core, z = me % NC, me // (NC * NY)
    me_s = me.reshape(1)
    tp_s = tp.reshape(1)
    c = key_head_scale * (LOG2E / math.sqrt(HEAD))

    row = retained[0, 0] * BLOCK
    own = jnp.concatenate(
        [lax.dynamic_slice_in_dim(part, row, BLOCK, 0) for part in (keys, values)], 0
    )
    planes = [[sid(z_, y_, c_) for z_ in range(NZ)] for y_ in range(NY) for c_ in range(NC)]
    stack = lax.all_to_all(
        jnp.broadcast_to(own, (NZ, SLOT, HEAD)), "seq", 0, 0, axis_index_groups=planes
    )
    holders = [sid(z_, NY - 1, 1) for z_ in range(NZ)]
    anchor = jnp.concatenate([keys[:BLOCK], values[:BLOCK]], 0)
    far = lax.ppermute(anchor, "seq", [(0, holders[3])])
    anchor = pl.pallas_call(
        choose_kernel,
        out_shape=jax.ShapeDtypeStruct((SLOT, HEAD), BF16),
        in_specs=[SMEM] + [VMEM] * 2,
        out_specs=VMEM,
        compiler_params=params(),
        cost_estimate=pl.CostEstimate(flops=1 << 33, bytes_accessed=1 << 17, transcendentals=0),
        name="choose_anchor",
    )(me_s, anchor, far)
    near = lax.ppermute(anchor, "seq", [(0, holders[1]), (holders[3], holders[2])])
    other_queries = lax.ppermute(queries, "seq", [(sid(*s), sid(s[0], s[1], 1 - s[2])) for s in PLACES])
    placed = jnp.where(jnp.logical_or(me == holders[1], me == holders[2]), near, anchor)
    holds = jnp.where(z == 0, me == 0, me % (NY * NC) == NY * NC - 1)
    block = jnp.concatenate(
        [stack[: NZ - 1].reshape(MSG - SLOT, HEAD), jnp.where(holds, placed, stack[NZ - 1])], 0
    )

    fwd = [lax.ppermute(block, "seq", y_perm(1))]
    bwd = [lax.ppermute(block, "seq", y_perm(-1))]
    for _ in range(2):
        fwd.append(lax.ppermute(fwd[-1], "seq", y_perm(1)))
        bwd.append(lax.ppermute(bwd[-1], "seq", y_perm(-1)))
    turn = [(sid(z_, y_, c_), sid(z_, y_ + (1 if c_ == 0 else -1), c_)) for z_, y_, c_ in PLACES]
    half = lax.ppermute(jnp.where(core == 0, fwd[-1], bwd[-1]), "seq", turn)

    state_shapes = [M_SHAPE, ACC_SHAPE, M_SHAPE, ACC_SHAPE]
    m0, a0 = pl.pallas_call(
        local_kernel,
        out_shape=[M_SHAPE, ACC_SHAPE],
        in_specs=[SMEM] + [VMEM] * 3,
        out_specs=[VMEM] * 2,
        scratch_shapes=[pltpu.VMEM((TOK, 2 * HEAD), BF16)],
        compiler_params=params(),
        cost_estimate=cost(512, 1),
        name="attend_local",
    )(c, queries, keys, values)
    state = pl.pallas_call(
        chip_kernel,
        out_shape=state_shapes,
        in_specs=[SMEM, SMEM] + [VMEM] * 5,
        out_specs=[VMEM] * 4,
        scratch_shapes=scratch(4),
        input_output_aliases={5: 0, 6: 1},
        compiler_params=params(),
        cost_estimate=cost(512, 2),
        name="attend_own_chip",
    )(me_s, c, queries, other_queries, block, m0, a0)
    for step in range(1, 4):
        state = pl.pallas_call(
            functools.partial(ring_kernel, step),
            out_shape=state_shapes,
            in_specs=[SMEM, SMEM] + [VMEM] * 8,
            out_specs=[VMEM] * 4,
            scratch_shapes=[pltpu.VMEM((2 * MSG, HEAD), BF16)] + scratch(8),
            input_output_aliases={6: 0, 7: 1, 8: 2, 9: 3},
            compiler_params=params(),
            cost_estimate=cost(1024, 2),
            name="attend_ring",
        )(me_s, c, queries, other_queries, fwd[step - 1], bwd[step - 1], *state)
    m0, a0, m1, a1 = state
    message, _, _ = pl.pallas_call(
        functools.partial(last_kernel, True),
        out_shape=[jax.ShapeDtypeStruct((HEADS, TOK, 2 * HEAD), BF16), M_SHAPE, ACC_SHAPE],
        in_specs=[SMEM, SMEM] + [VMEM] * 4,
        out_specs=[VMEM] * 3,
        scratch_shapes=scratch(4),
        input_output_aliases={4: 1, 5: 2},
        compiler_params=params(),
        cost_estimate=cost(512, 1),
        name="attend_last_other",
    )(me_s, c, other_queries, half, m1, a1)
    got = lax.ppermute(message, "seq", [(sid(*s), sid(s[0], s[1], 1 - s[2])) for s in PLACES])
    m0, a0 = pl.pallas_call(
        functools.partial(last_kernel, False),
        out_shape=[M_SHAPE, ACC_SHAPE],
        in_specs=[SMEM, SMEM] + [VMEM] * 4,
        out_specs=[VMEM] * 2,
        scratch_shapes=scratch(4),
        input_output_aliases={4: 0, 5: 1},
        compiler_params=params(),
        cost_estimate=cost(512, 1),
        name="attend_last_own",
    )(me_s, c, queries, half, m0, a0)

    wide_cols = out_weight.shape[1] // (NX * NH)

    block_shape = jax.ShapeDtypeStruct((TOK, wide_cols), BF16)
    att, there = pl.pallas_call(
        merge_kernel,
        out_shape=[
            jax.ShapeDtypeStruct((TOK, HEADS * HEAD), BF16),
            jax.ShapeDtypeStruct((NX, TOK, wide_cols), BF16),
        ],
        in_specs=[SMEM] + [VMEM] * 4,
        out_specs=[VMEM] * 2,
        compiler_params=params(),
        cost_estimate=pl.CostEstimate(flops=1 << 31, bytes_accessed=8 << 20, transcendentals=1 << 18),
        name="merge_project",
    )(tp_s, m0, a0, got, out_weight)
    rows = [[h * NX + x for x in range(NX)] for h in range(NH)]
    swap = [(i, (i + NX) % (NX * NH)) for i in range(NX * NH)]
    there = lax.all_to_all(there, "tp", 0, 0, axis_index_groups=rows)
    here = pl.pallas_call(
        own_kernel,
        out_shape=[block_shape] * NX,
        in_specs=[SMEM] + [VMEM] * 2,
        out_specs=[VMEM] * NX,
        compiler_params=params(),
        cost_estimate=pl.CostEstimate(flops=1 << 31, bytes_accessed=2 << 20, transcendentals=0),
        name="project_own_half",
    )(tp_s, att, out_weight)
    there, *parts = pl.pallas_call(
        sum_kernel,
        out_shape=[block_shape] * NX,
        in_specs=[VMEM] * NX,
        out_specs=[VMEM] * NX,
        compiler_params=params(),
        name="sum_other_half",
    )(there, *here[1:])
    parts = [
        lax.ppermute(part, "tp", [(i, i // NX * NX + (i + k) % NX) for i in range(NX * NH)])
        for k, part in enumerate(parts, 1)
    ]
    part = pl.pallas_call(
        add_kernel,
        out_shape=jax.ShapeDtypeStruct((TOK, wide_cols), F32),
        in_specs=[VMEM] * 2,
        out_specs=VMEM,
        compiler_params=params(),
        cost_estimate=pl.CostEstimate(flops=1 << 33, bytes_accessed=1 << 20, transcendentals=0),
        name="add_crossed",
    )(here[0], lax.ppermute(there, "tp", swap))
    projected, squares = pl.pallas_call(
        square_kernel,
        out_shape=[
            jax.ShapeDtypeStruct((TOK, wide_cols), F32),
            jax.ShapeDtypeStruct((NX * NH, 8, TOK), F32),
        ],
        in_specs=[VMEM] * NX,
        out_specs=[VMEM] * 2,
        compiler_params=params(),
        name="sum_and_square",
    )(part, *parts)
    squares = lax.all_to_all(squares, "tp", 0, 0)
    return pl.pallas_call(
        functools.partial(norm_kernel, out_weight.shape[1]),
        out_shape=jax.ShapeDtypeStruct((TOK, wide_cols), BF16),
        in_specs=[VMEM] * 3,
        out_specs=VMEM,
        compiler_params=params(),
        name="normalize",
    )(projected, squares, norm_gain.reshape(1, wide_cols))


def solution(mesh):
    return jax.shard_map(
        shards,
        mesh=mesh,
        in_specs=(
            P("seq", "tp"),
            P("seq", "tp"),
            P("seq", "tp"),
            P("tp"),
            P("seq", None),
            P("tp", None),
            P("tp"),
        ),
        out_specs=P("seq", "tp"),
        check_vma=False,
    )
```

```python
import functools
import math

import jax
import jax.numpy as jnp
from jax import lax
from jax.experimental import pallas as pl
from jax.experimental.pallas import tpu as pltpu
from jax.sharding import PartitionSpec as P

HEAD = 128
BLOCK = 128
LOG2E = math.log2(math.e)
NZ, NY, NC = 4, 8, 2
NX, NH = 4, 2
HEADS = 4
TOK = 256
SLOT = 2 * BLOCK
MSG = NZ * SLOT
LOW = -1e30
F32 = jnp.float32
BF16 = jnp.bfloat16

SMEM = pl.BlockSpec(memory_space=pltpu.SMEM)
VMEM = pl.BlockSpec(memory_space=pltpu.VMEM)
M_SHAPE = jax.ShapeDtypeStruct((HEADS, TOK, HEAD), F32)
ACC_SHAPE = jax.ShapeDtypeStruct((HEADS, TOK, 2 * HEAD), F32)


def sid(z, y, c):
    return (z * NY + y % NY) * NC + c


PLACES = [(z, y, c) for z in range(NZ) for y in range(NY) for c in range(NC)]


def y_perm(k):
    return [(sid(z, y, c), sid(z, y + k, c)) for z, y, c in PLACES]


def cross(a, b):
    return lax.dot_general(a, b, (((1,), (1,)), ((), ())), preferred_element_type=F32)


def plain(a, b):
    return lax.dot_general(a, b, (((1,), (0,)), ((), ())), preferred_element_type=F32)


def wide(a, n):
    return jnp.concatenate([a] * n, axis=1)


def seen(me, query_core, key_y):
    z, y, core = me // (NY * NC), (me // NC) % NY, me % NC
    holder_y = jnp.where(z == 0, 0, NY - 1)
    holder_core = jnp.where(z == 0, 0, 1)
    anchor = jnp.logical_and(core == holder_core, key_y == holder_y)
    first_piece = (z * NY + y) * NC + query_core == 0
    below = jnp.logical_or(key_y < y, jnp.logical_and(key_y == y, core < query_core)).astype(jnp.int32)
    flags = [jnp.where(j == z, below, (j < z).astype(jnp.int32)) for j in range(NZ)]
    flags[-1] = jnp.where(anchor, jnp.logical_not(first_piece).astype(jnp.int32), flags[-1])
    return flags


def prepare(blocks, shown, kk, vv):
    first = jnp.int32(0)
    for j in reversed(range(len(shown))):
        first = jnp.where(shown[j] > 0, j, first)
    for j, flag in enumerate(shown):
        src = jnp.where(flag > 0, j, first)
        rows = pl.multiple_of(src * SLOT, SLOT)
        kk[pl.ds(j * BLOCK, BLOCK), :] = blocks[pl.ds(rows, BLOCK), :]
        scale = flag.astype(F32)
        v = blocks[pl.ds(j * SLOT + BLOCK, BLOCK), :].astype(F32) * scale
        vv[pl.ds(j * BLOCK, BLOCK), 0:HEAD] = v.astype(BF16)
        vv[pl.ds(j * BLOCK, BLOCK), HEAD : 2 * HEAD] = jnp.full((BLOCK, HEAD), scale, F32).astype(BF16)


def attend_heads(c, q_ref, kk, vv, m_ref, acc_ref):
    def scores(h):
        return cross(q_ref[:, h * HEAD : (h + 1) * HEAD], kk[...])

    s = scores(0)
    for h in range(HEADS):
        later = scores(h + 1) if h + 1 < HEADS else None
        s = s * c
        m_old = m_ref[h]
        m_new = jnp.maximum(m_old, jnp.max(s, axis=1, keepdims=True))
        alpha = jnp.exp2(m_old - m_new)
        p = jnp.exp2(s - wide(m_new, s.shape[1] // HEAD)).astype(BF16)
        m_ref[h] = m_new
        acc_ref[h] = acc_ref[h] * wide(alpha, 2) + plain(p, vv[...])
        s = later


def shown_slots(me, core, key_ys):
    shown = []
    for key_y in key_ys:
        shown += seen(me, core, key_y)
    return shown, functools.reduce(lambda a, b: a + b, shown)


def attend_set(me, core, key_ys, c, q_ref, blocks, kk, vv, m_ref, acc_ref):
    shown, total = shown_slots(me, core, key_ys)

    @pl.when(total > 0)
    def _():
        prepare(blocks, shown, kk, vv)
        attend_heads(c, q_ref, kk, vv, m_ref, acc_ref)


def attend_both(me, key_ys, c, sets, blocks, kk, vv):
    core = me % NC
    for i, (q_ref, m_ref, acc_ref) in enumerate(sets):
        shown, total = shown_slots(me, 1 - core if i else core, key_ys)
        fresh = total > 0
        if i:
            fresh = jnp.logical_and(fresh, me // NC == 0)

        @pl.when(fresh)
        def _():
            prepare(blocks, shown, kk, vv)

        @pl.when(total > 0)
        def _():
            attend_heads(c, q_ref, kk, vv, m_ref, acc_ref)


def local_kernel(c_ref, q, k, v, m, a, lv):
    lv[:, 0:HEAD] = v[...]
    lv[:, HEAD : 2 * HEAD] = jnp.ones((TOK, HEAD), BF16)
    c = c_ref[0]
    row = lax.broadcasted_iota(jnp.int32, (TOK, TOK), 0)
    col = lax.broadcasted_iota(jnp.int32, (TOK, TOK), 1)
    for h in range(HEADS):
        s = cross(q[:, h * HEAD : (h + 1) * HEAD], k[...]) * c
        s = jnp.where(row >= col, s, LOW)
        top = jnp.broadcast_to(jnp.max(s, axis=1, keepdims=True), (TOK, HEAD))
        p = jnp.exp2(s - wide(top, TOK // HEAD)).astype(BF16)
        a[h] = plain(p, lv[...])
        m[h] = top


def chip_kernel(me_ref, c_ref, q0, q1, blk, m0i, a0i, m0, a0, m1, a1, kk, vv):
    me = me_ref[0]
    c = c_ref[0]
    core = me % NC
    y = (me // NC) % NY
    m0[...] = m0i[...]
    a0[...] = a0i[...]
    m1[...] = jnp.full(m1.shape, LOW, F32)
    a1[...] = jnp.zeros(a1.shape, F32)
    attend_set(me, core, [y], c, q0, blk, kk, vv, m0, a0)
    attend_set(me, 1 - core, [y], c, q1, blk, kk, vv, m1, a1)


def ring_kernel(step, me_ref, c_ref, q0, q1, fwd, bwd, m0i, a0i, m1i, a1i, m0, a0, m1, a1, blocks, kk, vv):
    me = me_ref[0]
    c = c_ref[0]
    y = (me // NC) % NY
    m0[...] = m0i[...]
    a0[...] = a0i[...]
    m1[...] = m1i[...]
    a1[...] = a1i[...]
    blocks[0:MSG, :] = fwd[...]
    blocks[MSG : 2 * MSG, :] = bwd[...]
    key_ys = [(y + NY - step) % NY, (y + step) % NY]
    attend_both(me, key_ys, c, ((q0, m0, a0), (q1, m1, a1)), blocks, kk, vv)


def last_kernel(other, me_ref, c_ref, q, blk, mi, ai, *rest):
    if other:
        out, m, a, kk, vv = rest
    else:
        m, a, kk, vv = rest
    me = me_ref[0]
    core = me % NC
    y = (me // NC) % NY
    m[...] = mi[...]
    a[...] = ai[...]
    key_ys = [(y + NY // 2) % NY]
    attend_set(me, 1 - core if other else core, key_ys, c_ref[0], q, blk, kk, vv, m, a)
    if other:
        lane = lax.broadcasted_iota(jnp.int32, (TOK, HEAD), 1)
        for h in range(HEADS):
            total = a[h][:, HEAD:]
            some = total > 0.0
            safe = jnp.where(some, total, 1.0)
            out[h, :, 0:HEAD] = (a[h][:, :HEAD] / safe).astype(BF16)
            lse = jnp.where(some, m[h] + jnp.log2(safe), LOW)
            hi = lse.astype(BF16).astype(F32)
            mid = (lse - hi).astype(BF16).astype(F32)
            low = lse - hi - mid
            parts = jnp.where(lane == 0, hi, jnp.where(lane == 1, mid, low))
            out[h, :, HEAD : 2 * HEAD] = parts.astype(BF16)


def project(att, w, half, j, cols):
    return plain(att[...], w[:, pl.ds(pl.multiple_of((half * NX + j) * cols, cols), cols)]).astype(BF16)


def merge_kernel(tp_ref, m, a, got, w, att, there):
    for h in range(HEADS):
        parts = got[h][:, HEAD:].astype(F32)
        lse = (parts[:, 0:1] + parts[:, 1:2]) + parts[:, 2:3]
        mine = m[h]
        top = jnp.maximum(mine, lse)
        w0 = jnp.exp2(mine - top)
        w1 = jnp.exp2(lse - top)
        acc = a[h][:, :HEAD] * w0 + got[h][:, :HEAD].astype(F32) * w1
        total = a[h][:, HEAD:] * w0 + w1
        att[:, h * HEAD : (h + 1) * HEAD] = (acc / total).astype(BF16)
    for j in range(NX):
        there[j] = project(att, w, 1 - tp_ref[0] // NX, j, there.shape[2])


def own_kernel(tp_ref, att, w, *outs):
    x, half = tp_ref[0] % NX, tp_ref[0] // NX
    for k, out in enumerate(outs):
        out[...] = project(att, w, half, (x + k) % NX, out.shape[1])


def sum_kernel(parts, out):
    total = parts[0].astype(F32)
    for j in range(1, NX):
        total += parts[j].astype(F32)
    out[...] = total.astype(BF16)


def choose_kernel(me_ref, here, there, out):
    last = me_ref[0] == NZ * NY * NC - 1

    @pl.when(last)
    def _():
        out[...] = there[...]

    @pl.when(jnp.logical_not(last))
    def _():
        out[...] = here[...]


def square_kernel(*refs):
    *parts, out, squares = refs
    total = parts[0][...].astype(F32)
    for part in parts[1:]:
        total += part[...].astype(F32)
    out[...] = total
    ones = jnp.ones((8, total.shape[1]), F32)
    sums = lax.dot_general(
        ones,
        total * total,
        (((1,), (1,)), ((), ())),
        precision=lax.Precision.HIGHEST,
        preferred_element_type=F32,
    )
    for j in range(NX * NH):
        squares[j] = sums


def norm_kernel(features, projected, squares, gain, out):
    total = squares[0]
    for j in range(1, NX * NH):
        total += squares[j]
    scale = lax.rsqrt(jnp.transpose(total)[:, 0:1] / features + 1e-05)
    out[...] = (projected[...] * scale * gain[...]).astype(BF16)


def params(mib=20):
    return pltpu.CompilerParams(vmem_limit_bytes=mib << 20)


def scratch(n):
    return [pltpu.VMEM((n * BLOCK, HEAD), BF16), pltpu.VMEM((n * BLOCK, 2 * HEAD), BF16)]


def cost(keys, sets):
    rows = HEADS * TOK * sets
    return pl.CostEstimate(
        flops=rows * keys * HEAD * 20, bytes_accessed=4 << 20, transcendentals=rows * keys
    )


def shards(queries, keys, values, key_head_scale, retained, out_weight, norm_gain):
    me = lax.axis_index("seq").astype(jnp.int32)
    tp = lax.axis_index("tp").astype(jnp.int32)
    core, z = me % NC, me // (NC * NY)
    me_s = me.reshape(1)
    tp_s = tp.reshape(1)
    c = key_head_scale * (LOG2E / math.sqrt(HEAD))

    row = retained[0, 0] * BLOCK
    own = jnp.concatenate(
        [lax.dynamic_slice_in_dim(part, row, BLOCK, 0) for part in (keys, values)], 0
    )
    planes = [[sid(z_, y_, c_) for z_ in range(NZ)] for y_ in range(NY) for c_ in range(NC)]
    stack = lax.all_to_all(
        jnp.broadcast_to(own, (NZ, SLOT, HEAD)), "seq", 0, 0, axis_index_groups=planes
    )
    holders = [sid(z_, NY - 1, 1) for z_ in range(NZ)]
    anchor = jnp.concatenate([keys[:BLOCK], values[:BLOCK]], 0)
    far = lax.ppermute(anchor, "seq", [(0, holders[3])])
    anchor = pl.pallas_call(
        choose_kernel,
        out_shape=jax.ShapeDtypeStruct((SLOT, HEAD), BF16),
        in_specs=[SMEM] + [VMEM] * 2,
        out_specs=VMEM,
        compiler_params=params(),
        cost_estimate=pl.CostEstimate(flops=1 << 33, bytes_accessed=1 << 17, transcendentals=0),
        name="choose_anchor",
    )(me_s, anchor, far)
    near = lax.ppermute(anchor, "seq", [(0, holders[1]), (holders[3], holders[2])])
    other_queries = lax.ppermute(queries, "seq", [(sid(*s), sid(s[0], s[1], 1 - s[2])) for s in PLACES])
    placed = jnp.where(jnp.logical_or(me == holders[1], me == holders[2]), near, anchor)
    holds = jnp.where(z == 0, me == 0, me % (NY * NC) == NY * NC - 1)
    block = jnp.concatenate(
        [stack[: NZ - 1].reshape(MSG - SLOT, HEAD), jnp.where(holds, placed, stack[NZ - 1])], 0
    )

    fwd = [lax.ppermute(block, "seq", y_perm(1))]
    bwd = [lax.ppermute(block, "seq", y_perm(-1))]
    for _ in range(2):
        fwd.append(lax.ppermute(fwd[-1], "seq", y_perm(1)))
        bwd.append(lax.ppermute(bwd[-1], "seq", y_perm(-1)))
    turn = [(sid(z_, y_, c_), sid(z_, y_ + (1 if c_ == 0 else -1), c_)) for z_, y_, c_ in PLACES]
    half = lax.ppermute(jnp.where(core == 0, fwd[-1], bwd[-1]), "seq", turn)

    state_shapes = [M_SHAPE, ACC_SHAPE, M_SHAPE, ACC_SHAPE]
    m0, a0 = pl.pallas_call(
        local_kernel,
        out_shape=[M_SHAPE, ACC_SHAPE],
        in_specs=[SMEM] + [VMEM] * 3,
        out_specs=[VMEM] * 2,
        scratch_shapes=[pltpu.VMEM((TOK, 2 * HEAD), BF16)],
        compiler_params=params(),
        cost_estimate=cost(512, 1),
        name="attend_local",
    )(c, queries, keys, values)
    state = pl.pallas_call(
        chip_kernel,
        out_shape=state_shapes,
        in_specs=[SMEM, SMEM] + [VMEM] * 5,
        out_specs=[VMEM] * 4,
        scratch_shapes=scratch(4),
        input_output_aliases={5: 0, 6: 1},
        compiler_params=params(),
        cost_estimate=cost(512, 2),
        name="attend_own_chip",
    )(me_s, c, queries, other_queries, block, m0, a0)
    for step in range(1, 4):
        state = pl.pallas_call(
            functools.partial(ring_kernel, step),
            out_shape=state_shapes,
            in_specs=[SMEM, SMEM] + [VMEM] * 8,
            out_specs=[VMEM] * 4,
            scratch_shapes=[pltpu.VMEM((2 * MSG, HEAD), BF16)] + scratch(8),
            input_output_aliases={6: 0, 7: 1, 8: 2, 9: 3},
            compiler_params=params(),
            cost_estimate=cost(1024, 2),
            name="attend_ring",
        )(me_s, c, queries, other_queries, fwd[step - 1], bwd[step - 1], *state)
    m0, a0, m1, a1 = state
    message, _, _ = pl.pallas_call(
        functools.partial(last_kernel, True),
        out_shape=[jax.ShapeDtypeStruct((HEADS, TOK, 2 * HEAD), BF16), M_SHAPE, ACC_SHAPE],
        in_specs=[SMEM, SMEM] + [VMEM] * 4,
        out_specs=[VMEM] * 3,
        scratch_shapes=scratch(4),
        input_output_aliases={4: 1, 5: 2},
        compiler_params=params(),
        cost_estimate=cost(512, 1),
        name="attend_last_other",
    )(me_s, c, other_queries, half, m1, a1)
    got = lax.ppermute(message, "seq", [(sid(*s), sid(s[0], s[1], 1 - s[2])) for s in PLACES])
    m0, a0 = pl.pallas_call(
        functools.partial(last_kernel, False),
        out_shape=[M_SHAPE, ACC_SHAPE],
        in_specs=[SMEM, SMEM] + [VMEM] * 4,
        out_specs=[VMEM] * 2,
        scratch_shapes=scratch(4),
        input_output_aliases={4: 0, 5: 1},
        compiler_params=params(),
        cost_estimate=cost(512, 1),
        name="attend_last_own",
    )(me_s, c, queries, half, m0, a0)

    wide_cols = out_weight.shape[1] // (NX * NH)

    block_shape = jax.ShapeDtypeStruct((TOK, wide_cols), BF16)
    att, there = pl.pallas_call(
        merge_kernel,
        out_shape=[
            jax.ShapeDtypeStruct((TOK, HEADS * HEAD), BF16),
            jax.ShapeDtypeStruct((NX, TOK, wide_cols), BF16),
        ],
        in_specs=[SMEM] + [VMEM] * 4,
        out_specs=[VMEM] * 2,
        compiler_params=params(),
        cost_estimate=pl.CostEstimate(flops=1 << 31, bytes_accessed=8 << 20, transcendentals=1 << 18),
        name="merge_project",
    )(tp_s, m0, a0, got, out_weight)
    rows = [[h * NX + x for x in range(NX)] for h in range(NH)]
    swap = [(i, (i + NX) % (NX * NH)) for i in range(NX * NH)]
    there = lax.all_to_all(there, "tp", 0, 0, axis_index_groups=rows)
    here = pl.pallas_call(
        own_kernel,
        out_shape=[block_shape] * NX,
        in_specs=[SMEM] + [VMEM] * 2,
        out_specs=[VMEM] * NX,
        compiler_params=params(),
        cost_estimate=pl.CostEstimate(flops=1 << 31, bytes_accessed=2 << 20, transcendentals=0),
        name="project_own_half",
    )(tp_s, att, out_weight)
    parts = [here[0]] + [
        lax.ppermute(here[k], "tp", [(i, i // NX * NX + (i + k) % NX) for i in range(NX * NH)])
        for k in range(1, NX)
    ]
    there = pl.pallas_call(
        sum_kernel,
        out_shape=block_shape,
        in_specs=[VMEM],
        out_specs=VMEM,
        compiler_params=params(),
        name="sum_other_half",
    )(there)
    parts.append(lax.ppermute(there, "tp", swap))
    projected, squares = pl.pallas_call(
        square_kernel,
        out_shape=[
            jax.ShapeDtypeStruct((TOK, wide_cols), F32),
            jax.ShapeDtypeStruct((NX * NH, 8, TOK), F32),
        ],
        in_specs=[VMEM] * (NX + 1),
        out_specs=[VMEM] * 2,
        compiler_params=params(),
        name="sum_and_square",
    )(*parts)
    squares = lax.all_to_all(squares, "tp", 0, 0)
    return pl.pallas_call(
        functools.partial(norm_kernel, out_weight.shape[1]),
        out_shape=jax.ShapeDtypeStruct((TOK, wide_cols), BF16),
        in_specs=[VMEM] * 3,
        out_specs=VMEM,
        compiler_params=params(),
        name="normalize",
    )(projected, squares, norm_gain.reshape(1, wide_cols))


def solution(mesh):
    return jax.shard_map(
        shards,
        mesh=mesh,
        in_specs=(
            P("seq", "tp"),
            P("seq", "tp"),
            P("seq", "tp"),
            P("tp"),
            P("seq", None),
            P("tp", None),
            P("tp"),
        ),
        out_specs=P("seq", "tp"),
        check_vma=False,
    )
```

```python
import functools
import math

import jax
import jax.numpy as jnp
from jax import lax
from jax.experimental import pallas as pl
from jax.experimental.pallas import tpu as pltpu
from jax.sharding import PartitionSpec as P

HEAD = 128
BLOCK = 128
LOG2E = math.log2(math.e)
NZ, NY, NC = 4, 8, 2
NX, NH = 4, 2
HEADS = 4
TOK = 256
SLOT = 2 * BLOCK
MSG = NZ * SLOT
LOW = -1e30
F32 = jnp.float32
BF16 = jnp.bfloat16

SMEM = pl.BlockSpec(memory_space=pltpu.SMEM)
VMEM = pl.BlockSpec(memory_space=pltpu.VMEM)
M_SHAPE = jax.ShapeDtypeStruct((HEADS, TOK, HEAD), F32)
ACC_SHAPE = jax.ShapeDtypeStruct((HEADS, TOK, 2 * HEAD), F32)


def sid(z, y, c):
    return (z * NY + y % NY) * NC + c


PLACES = [(z, y, c) for z in range(NZ) for y in range(NY) for c in range(NC)]


def y_perm(k):
    return [(sid(z, y, c), sid(z, y + k, c)) for z, y, c in PLACES]


def cross(a, b):
    return lax.dot_general(a, b, (((1,), (1,)), ((), ())), preferred_element_type=F32)


def plain(a, b):
    return lax.dot_general(a, b, (((1,), (0,)), ((), ())), preferred_element_type=F32)


def wide(a, n):
    return jnp.concatenate([a] * n, axis=1)


def seen(me, query_core, key_y):
    z, y, core = me // (NY * NC), (me // NC) % NY, me % NC
    holder_y = jnp.where(z == 0, 0, NY - 1)
    holder_core = jnp.where(z == 0, 0, 1)
    anchor = jnp.logical_and(core == holder_core, key_y == holder_y)
    first_piece = (z * NY + y) * NC + query_core == 0
    below = jnp.logical_or(key_y < y, jnp.logical_and(key_y == y, core < query_core)).astype(jnp.int32)
    flags = [jnp.where(j == z, below, (j < z).astype(jnp.int32)) for j in range(NZ)]
    flags[-1] = jnp.where(anchor, jnp.logical_not(first_piece).astype(jnp.int32), flags[-1])
    return flags


def prepare(blocks, shown, kk, vv):
    first = jnp.int32(0)
    for j in reversed(range(len(shown))):
        first = jnp.where(shown[j] > 0, j, first)
    for j, flag in enumerate(shown):
        src = jnp.where(flag > 0, j, first)
        rows = pl.multiple_of(src * SLOT, SLOT)
        kk[pl.ds(j * BLOCK, BLOCK), :] = blocks[pl.ds(rows, BLOCK), :]
        scale = flag.astype(F32)
        v = blocks[pl.ds(j * SLOT + BLOCK, BLOCK), :].astype(F32) * scale
        vv[pl.ds(j * BLOCK, BLOCK), 0:HEAD] = v.astype(BF16)
        vv[pl.ds(j * BLOCK, BLOCK), HEAD : 2 * HEAD] = jnp.full((BLOCK, HEAD), scale, F32).astype(BF16)


def attend_heads(c, q_ref, kk, vv, m_ref, acc_ref):
    def scores(h):
        return cross(q_ref[:, h * HEAD : (h + 1) * HEAD], kk[...])

    s = scores(0)
    for h in range(HEADS):
        later = scores(h + 1) if h + 1 < HEADS else None
        s = s * c
        m_old = m_ref[h]
        m_new = jnp.maximum(m_old, jnp.max(s, axis=1, keepdims=True))
        alpha = jnp.exp2(m_old - m_new)
        p = jnp.exp2(s - wide(m_new, s.shape[1] // HEAD)).astype(BF16)
        m_ref[h] = m_new
        acc_ref[h] = acc_ref[h] * wide(alpha, 2) + plain(p, vv[...])
        s = later


def shown_slots(me, core, key_ys):
    shown = []
    for key_y in key_ys:
        shown += seen(me, core, key_y)
    return shown, functools.reduce(lambda a, b: a + b, shown)


def attend_set(me, core, key_ys, c, q_ref, blocks, kk, vv, m_ref, acc_ref):
    shown, total = shown_slots(me, core, key_ys)

    @pl.when(total > 0)
    def _():
        prepare(blocks, shown, kk, vv)
        attend_heads(c, q_ref, kk, vv, m_ref, acc_ref)


def attend_both(me, key_ys, c, sets, blocks, kk, vv):
    core = me % NC
    for i, (q_ref, m_ref, acc_ref) in enumerate(sets):
        shown, total = shown_slots(me, 1 - core if i else core, key_ys)
        fresh = total > 0
        if i:
            fresh = jnp.logical_and(fresh, me // NC == 0)

        @pl.when(fresh)
        def _():
            prepare(blocks, shown, kk, vv)

        @pl.when(total > 0)
        def _():
            attend_heads(c, q_ref, kk, vv, m_ref, acc_ref)


def local_kernel(c_ref, q, k, v, m, a, lv):
    lv[:, 0:HEAD] = v[...]
    lv[:, HEAD : 2 * HEAD] = jnp.ones((TOK, HEAD), BF16)
    c = c_ref[0]
    row = lax.broadcasted_iota(jnp.int32, (TOK, TOK), 0)
    col = lax.broadcasted_iota(jnp.int32, (TOK, TOK), 1)
    for h in range(HEADS):
        s = cross(q[:, h * HEAD : (h + 1) * HEAD], k[...]) * c
        s = jnp.where(row >= col, s, LOW)
        top = jnp.broadcast_to(jnp.max(s, axis=1, keepdims=True), (TOK, HEAD))
        p = jnp.exp2(s - wide(top, TOK // HEAD)).astype(BF16)
        a[h] = plain(p, lv[...])
        m[h] = top


def chip_kernel(me_ref, c_ref, q0, q1, blk, m0i, a0i, m0, a0, m1, a1, kk, vv):
    me = me_ref[0]
    c = c_ref[0]
    core = me % NC
    y = (me // NC) % NY
    m0[...] = m0i[...]
    a0[...] = a0i[...]
    m1[...] = jnp.full(m1.shape, LOW, F32)
    a1[...] = jnp.zeros(a1.shape, F32)
    attend_set(me, core, [y], c, q0, blk, kk, vv, m0, a0)
    attend_set(me, 1 - core, [y], c, q1, blk, kk, vv, m1, a1)


def ring_kernel(step, me_ref, c_ref, q0, q1, fwd, bwd, m0i, a0i, m1i, a1i, m0, a0, m1, a1, blocks, kk, vv):
    me = me_ref[0]
    c = c_ref[0]
    y = (me // NC) % NY
    m0[...] = m0i[...]
    a0[...] = a0i[...]
    m1[...] = m1i[...]
    a1[...] = a1i[...]
    blocks[0:MSG, :] = fwd[...]
    blocks[MSG : 2 * MSG, :] = bwd[...]
    key_ys = [(y + NY - step) % NY, (y + step) % NY]
    attend_both(me, key_ys, c, ((q0, m0, a0), (q1, m1, a1)), blocks, kk, vv)


def last_kernel(other, me_ref, c_ref, q, blk, mi, ai, *rest):
    if other:
        out, m, a, kk, vv = rest
    else:
        m, a, kk, vv = rest
    me = me_ref[0]
    core = me % NC
    y = (me // NC) % NY
    m[...] = mi[...]
    a[...] = ai[...]
    key_ys = [(y + NY // 2) % NY]
    attend_set(me, 1 - core if other else core, key_ys, c_ref[0], q, blk, kk, vv, m, a)
    if other:
        lane = lax.broadcasted_iota(jnp.int32, (TOK, HEAD), 1)
        for h in range(HEADS):
            total = a[h][:, HEAD:]
            some = total > 0.0
            safe = jnp.where(some, total, 1.0)
            out[h, :, 0:HEAD] = (a[h][:, :HEAD] / safe).astype(BF16)
            lse = jnp.where(some, m[h] + jnp.log2(safe), LOW)
            hi = lse.astype(BF16).astype(F32)
            mid = (lse - hi).astype(BF16).astype(F32)
            low = lse - hi - mid
            parts = jnp.where(lane == 0, hi, jnp.where(lane == 1, mid, low))
            out[h, :, HEAD : 2 * HEAD] = parts.astype(BF16)


def project(att, w, half, j, cols):
    return plain(att[...], w[:, pl.ds(pl.multiple_of((half * NX + j) * cols, cols), cols)]).astype(BF16)


def merge_kernel(tp_ref, m, a, got, w, att, there):
    for h in range(HEADS):
        parts = got[h][:, HEAD:].astype(F32)
        lse = (parts[:, 0:1] + parts[:, 1:2]) + parts[:, 2:3]
        mine = m[h]
        top = jnp.maximum(mine, lse)
        w0 = jnp.exp2(mine - top)
        w1 = jnp.exp2(lse - top)
        acc = a[h][:, :HEAD] * w0 + got[h][:, :HEAD].astype(F32) * w1
        total = a[h][:, HEAD:] * w0 + w1
        att[:, h * HEAD : (h + 1) * HEAD] = (acc / total).astype(BF16)
    for j in range(NX):
        there[j] = project(att, w, 1 - tp_ref[0] // NX, j, there.shape[2])


def own_kernel(tp_ref, att, w, *outs):
    x, half = tp_ref[0] % NX, tp_ref[0] // NX
    for k, out in enumerate(outs):
        out[...] = project(att, w, half, (x + k) % NX, out.shape[1])


def sum_kernel(parts, out):
    total = parts[0].astype(F32)
    for j in range(1, NX):
        total += parts[j].astype(F32)
    out[...] = total.astype(BF16)


def choose_kernel(me_ref, here, there, out):
    last = me_ref[0] == NZ * NY * NC - 1

    @pl.when(last)
    def _():
        out[...] = there[...]

    @pl.when(jnp.logical_not(last))
    def _():
        out[...] = here[...]


def square_kernel(*refs):
    *parts, out, squares = refs
    total = parts[0][...].astype(F32)
    for part in parts[1:]:
        total += part[...].astype(F32)
    out[...] = total
    ones = jnp.ones((8, total.shape[1]), F32)
    sums = lax.dot_general(
        ones,
        total * total,
        (((1,), (1,)), ((), ())),
        precision=lax.Precision.HIGHEST,
        preferred_element_type=F32,
    )
    for j in range(NX * NH):
        squares[j] = sums


def norm_kernel(features, projected, squares, gain, out):
    total = squares[0]
    for j in range(1, NX * NH):
        total += squares[j]
    scale = lax.rsqrt(jnp.transpose(total)[:, 0:1] / features + 1e-05)
    out[...] = (projected[...] * scale * gain[...]).astype(BF16)


def params(mib=20):
    return pltpu.CompilerParams(vmem_limit_bytes=mib << 20)


def scratch(n):
    return [pltpu.VMEM((n * BLOCK, HEAD), BF16), pltpu.VMEM((n * BLOCK, 2 * HEAD), BF16)]


def cost(keys, sets):
    rows = HEADS * TOK * sets
    return pl.CostEstimate(
        flops=rows * keys * HEAD * 20, bytes_accessed=4 << 20, transcendentals=rows * keys
    )


def shards(queries, keys, values, key_head_scale, retained, out_weight, norm_gain):
    me = lax.axis_index("seq").astype(jnp.int32)
    tp = lax.axis_index("tp").astype(jnp.int32)
    z = me // (NC * NY)
    me_s = me.reshape(1)
    tp_s = tp.reshape(1)
    c = key_head_scale * (LOG2E / math.sqrt(HEAD))

    row = retained[0, 0] * BLOCK
    own = jnp.concatenate(
        [lax.dynamic_slice_in_dim(part, row, BLOCK, 0) for part in (keys, values)], 0
    )
    planes = [[sid(z_, y_, c_) for z_ in range(NZ)] for y_ in range(NY) for c_ in range(NC)]
    stack = lax.all_to_all(
        jnp.broadcast_to(own, (NZ, SLOT, HEAD)), "seq", 0, 0, axis_index_groups=planes
    )
    holders = [sid(z_, NY - 1, 1) for z_ in range(NZ)]
    anchor = jnp.concatenate([keys[:BLOCK], values[:BLOCK]], 0)
    far = lax.ppermute(anchor, "seq", [(0, holders[3])])
    other_queries = lax.ppermute(queries, "seq", [(sid(*s), sid(s[0], s[1], 1 - s[2])) for s in PLACES])
    anchor = pl.pallas_call(
        choose_kernel,
        out_shape=jax.ShapeDtypeStruct((SLOT, HEAD), BF16),
        in_specs=[SMEM] + [VMEM] * 2,
        out_specs=VMEM,
        compiler_params=params(),
        cost_estimate=pl.CostEstimate(flops=1 << 33, bytes_accessed=1 << 17, transcendentals=0),
        name="choose_anchor",
    )(me_s, anchor, far)
    near = lax.ppermute(anchor, "seq", [(0, holders[1]), (holders[3], holders[2])])
    placed = jnp.where(jnp.logical_or(me == holders[1], me == holders[2]), near, anchor)
    holds = jnp.where(z == 0, me == 0, me % (NY * NC) == NY * NC - 1)
    block = jnp.concatenate(
        [stack[: NZ - 1].reshape(MSG - SLOT, HEAD), jnp.where(holds, placed, stack[NZ - 1])], 0
    )

    fwd = [lax.ppermute(block, "seq", y_perm(1))]
    bwd = [lax.ppermute(block, "seq", y_perm(-1))]
    for _ in range(2):
        fwd.append(lax.ppermute(fwd[-1], "seq", y_perm(1)))
        bwd.append(lax.ppermute(bwd[-1], "seq", y_perm(-1)))
    half = lax.ppermute(fwd[-1], "seq", y_perm(1))

    state_shapes = [M_SHAPE, ACC_SHAPE, M_SHAPE, ACC_SHAPE]
    m0, a0 = pl.pallas_call(
        local_kernel,
        out_shape=[M_SHAPE, ACC_SHAPE],
        in_specs=[SMEM] + [VMEM] * 3,
        out_specs=[VMEM] * 2,
        scratch_shapes=[pltpu.VMEM((TOK, 2 * HEAD), BF16)],
        compiler_params=params(),
        cost_estimate=cost(512, 1),
        name="attend_local",
    )(c, queries, keys, values)
    state = pl.pallas_call(
        chip_kernel,
        out_shape=state_shapes,
        in_specs=[SMEM, SMEM] + [VMEM] * 5,
        out_specs=[VMEM] * 4,
        scratch_shapes=scratch(4),
        input_output_aliases={5: 0, 6: 1},
        compiler_params=params(),
        cost_estimate=cost(512, 2),
        name="attend_own_chip",
    )(me_s, c, queries, other_queries, block, m0, a0)
    for step in range(1, 4):
        state = pl.pallas_call(
            functools.partial(ring_kernel, step),
            out_shape=state_shapes,
            in_specs=[SMEM, SMEM] + [VMEM] * 8,
            out_specs=[VMEM] * 4,
            scratch_shapes=[pltpu.VMEM((2 * MSG, HEAD), BF16)] + scratch(8),
            input_output_aliases={6: 0, 7: 1, 8: 2, 9: 3},
            compiler_params=params(),
            cost_estimate=cost(1024, 2),
            name="attend_ring",
        )(me_s, c, queries, other_queries, fwd[step - 1], bwd[step - 1], *state)
    m0, a0, m1, a1 = state
    message, _, _ = pl.pallas_call(
        functools.partial(last_kernel, True),
        out_shape=[jax.ShapeDtypeStruct((HEADS, TOK, 2 * HEAD), BF16), M_SHAPE, ACC_SHAPE],
        in_specs=[SMEM, SMEM] + [VMEM] * 4,
        out_specs=[VMEM] * 3,
        scratch_shapes=scratch(4),
        input_output_aliases={4: 1, 5: 2},
        compiler_params=params(),
        cost_estimate=cost(512, 1),
        name="attend_last_other",
    )(me_s, c, other_queries, half, m1, a1)
    got = lax.ppermute(message, "seq", [(sid(*s), sid(s[0], s[1], 1 - s[2])) for s in PLACES])
    m0, a0 = pl.pallas_call(
        functools.partial(last_kernel, False),
        out_shape=[M_SHAPE, ACC_SHAPE],
        in_specs=[SMEM, SMEM] + [VMEM] * 4,
        out_specs=[VMEM] * 2,
        scratch_shapes=scratch(4),
        input_output_aliases={4: 0, 5: 1},
        compiler_params=params(),
        cost_estimate=cost(512, 1),
        name="attend_last_own",
    )(me_s, c, queries, half, m0, a0)

    wide_cols = out_weight.shape[1] // (NX * NH)

    block_shape = jax.ShapeDtypeStruct((TOK, wide_cols), BF16)
    att, there = pl.pallas_call(
        merge_kernel,
        out_shape=[
            jax.ShapeDtypeStruct((TOK, HEADS * HEAD), BF16),
            jax.ShapeDtypeStruct((NX, TOK, wide_cols), BF16),
        ],
        in_specs=[SMEM] + [VMEM] * 4,
        out_specs=[VMEM] * 2,
        compiler_params=params(),
        cost_estimate=pl.CostEstimate(flops=1 << 31, bytes_accessed=8 << 20, transcendentals=1 << 18),
        name="merge_project",
    )(tp_s, m0, a0, got, out_weight)
    rows = [[h * NX + x for x in range(NX)] for h in range(NH)]
    swap = [(i, (i + NX) % (NX * NH)) for i in range(NX * NH)]
    there = lax.all_to_all(there, "tp", 0, 0, axis_index_groups=rows)
    here = pl.pallas_call(
        own_kernel,
        out_shape=[block_shape] * NX,
        in_specs=[SMEM] + [VMEM] * 2,
        out_specs=[VMEM] * NX,
        compiler_params=params(),
        cost_estimate=pl.CostEstimate(flops=1 << 31, bytes_accessed=2 << 20, transcendentals=0),
        name="project_own_half",
    )(tp_s, att, out_weight)
    parts = [here[0]] + [
        lax.ppermute(here[k], "tp", [(i, i // NX * NX + (i + k) % NX) for i in range(NX * NH)])
        for k in range(1, NX)
    ]
    there = pl.pallas_call(
        sum_kernel,
        out_shape=block_shape,
        in_specs=[VMEM],
        out_specs=VMEM,
        compiler_params=params(),
        name="sum_other_half",
    )(there)
    parts.append(lax.ppermute(there, "tp", swap))
    projected, squares = pl.pallas_call(
        square_kernel,
        out_shape=[
            jax.ShapeDtypeStruct((TOK, wide_cols), F32),
            jax.ShapeDtypeStruct((NX * NH, 8, TOK), F32),
        ],
        in_specs=[VMEM] * (NX + 1),
        out_specs=[VMEM] * 2,
        compiler_params=params(),
        name="sum_and_square",
    )(*parts)
    squares = lax.all_to_all(squares, "tp", 0, 0)
    return pl.pallas_call(
        functools.partial(norm_kernel, out_weight.shape[1]),
        out_shape=jax.ShapeDtypeStruct((TOK, wide_cols), BF16),
        in_specs=[VMEM] * 3,
        out_specs=VMEM,
        compiler_params=params(),
        name="normalize",
    )(projected, squares, norm_gain.reshape(1, wide_cols))


def solution(mesh):
    return jax.shard_map(
        shards,
        mesh=mesh,
        in_specs=(
            P("seq", "tp"),
            P("seq", "tp"),
            P("seq", "tp"),
            P("tp"),
            P("seq", None),
            P("tp", None),
            P("tp"),
        ),
        out_specs=P("seq", "tp"),
        check_vma=False,
    )
```

```python
import functools
import math

import jax
import jax.numpy as jnp
from jax import lax
from jax.experimental import pallas as pl
from jax.experimental.pallas import tpu as pltpu
from jax.sharding import PartitionSpec as P

HEAD = 128
BLOCK = 128
LOG2E = math.log2(math.e)
NZ, NY, NC = 4, 8, 2
NX, NH = 4, 2
HEADS = 4
TOK = 256
SLOT = 2 * BLOCK
MSG = NZ * SLOT
LOW = -1e30
F32 = jnp.float32
BF16 = jnp.bfloat16

SMEM = pl.BlockSpec(memory_space=pltpu.SMEM)
VMEM = pl.BlockSpec(memory_space=pltpu.VMEM)
M_SHAPE = jax.ShapeDtypeStruct((HEADS, TOK, HEAD), F32)
ACC_SHAPE = jax.ShapeDtypeStruct((HEADS, TOK, 2 * HEAD), F32)


def sid(z, y, c):
    return (z * NY + y % NY) * NC + c


PLACES = [(z, y, c) for z in range(NZ) for y in range(NY) for c in range(NC)]


def y_perm(k):
    return [(sid(z, y, c), sid(z, y + k, c)) for z, y, c in PLACES]


def cross(a, b):
    return lax.dot_general(a, b, (((1,), (1,)), ((), ())), preferred_element_type=F32)


def plain(a, b):
    return lax.dot_general(a, b, (((1,), (0,)), ((), ())), preferred_element_type=F32)


def wide(a, n):
    return jnp.concatenate([a] * n, axis=1)


def seen(me, query_core, key_y):
    z, y, core = me // (NY * NC), (me // NC) % NY, me % NC
    holder_y = jnp.where(z == 0, 0, NY - 1)
    holder_core = jnp.where(z == 0, 0, 1)
    anchor = jnp.logical_and(core == holder_core, key_y == holder_y)
    first_piece = (z * NY + y) * NC + query_core == 0
    below = jnp.logical_or(key_y < y, jnp.logical_and(key_y == y, core < query_core)).astype(jnp.int32)
    flags = [jnp.where(j == z, below, (j < z).astype(jnp.int32)) for j in range(NZ)]
    flags[-1] = jnp.where(anchor, jnp.logical_not(first_piece).astype(jnp.int32), flags[-1])
    return flags


def prepare(blocks, shown, kk, vv):
    first = jnp.int32(0)
    for j in reversed(range(len(shown))):
        first = jnp.where(shown[j] > 0, j, first)
    for j, flag in enumerate(shown):
        src = jnp.where(flag > 0, j, first)
        rows = pl.multiple_of(src * SLOT, SLOT)
        kk[pl.ds(j * BLOCK, BLOCK), :] = blocks[pl.ds(rows, BLOCK), :]
        scale = flag.astype(F32)
        v = blocks[pl.ds(j * SLOT + BLOCK, BLOCK), :].astype(F32) * scale
        vv[pl.ds(j * BLOCK, BLOCK), 0:HEAD] = v.astype(BF16)
        vv[pl.ds(j * BLOCK, BLOCK), HEAD : 2 * HEAD] = jnp.full((BLOCK, HEAD), scale, F32).astype(BF16)


def attend_heads(c, q_ref, kk, vv, m_ref, acc_ref):
    def scores(h):
        return cross(q_ref[:, h * HEAD : (h + 1) * HEAD], kk[...])

    s = scores(0)
    for h in range(HEADS):
        later = scores(h + 1) if h + 1 < HEADS else None
        s = s * c
        m_old = m_ref[h]
        m_new = jnp.maximum(m_old, jnp.max(s, axis=1, keepdims=True))
        alpha = jnp.exp2(m_old - m_new)
        p = jnp.exp2(s - wide(m_new, s.shape[1] // HEAD)).astype(BF16)
        m_ref[h] = m_new
        acc_ref[h] = acc_ref[h] * wide(alpha, 2) + plain(p, vv[...])
        s = later


def shown_slots(me, core, key_ys):
    shown = []
    for key_y in key_ys:
        shown += seen(me, core, key_y)
    return shown, functools.reduce(lambda a, b: a + b, shown)


def attend_set(me, core, key_ys, c, q_ref, blocks, kk, vv, m_ref, acc_ref):
    shown, total = shown_slots(me, core, key_ys)

    @pl.when(total > 0)
    def _():
        prepare(blocks, shown, kk, vv)
        attend_heads(c, q_ref, kk, vv, m_ref, acc_ref)


def attend_both(me, key_ys, c, sets, blocks, kk, vv):
    core = me % NC
    for i, (q_ref, m_ref, acc_ref) in enumerate(sets):
        shown, total = shown_slots(me, 1 - core if i else core, key_ys)
        fresh = total > 0
        if i:
            fresh = jnp.logical_and(fresh, me // NC == 0)

        @pl.when(fresh)
        def _():
            prepare(blocks, shown, kk, vv)

        @pl.when(total > 0)
        def _():
            attend_heads(c, q_ref, kk, vv, m_ref, acc_ref)


def local_kernel(c_ref, q, k, v, m, a, lv):
    lv[:, 0:HEAD] = v[...]
    lv[:, HEAD : 2 * HEAD] = jnp.ones((TOK, HEAD), BF16)
    c = c_ref[0]
    row = lax.broadcasted_iota(jnp.int32, (TOK, TOK), 0)
    col = lax.broadcasted_iota(jnp.int32, (TOK, TOK), 1)
    for h in range(HEADS):
        s = cross(q[:, h * HEAD : (h + 1) * HEAD], k[...]) * c
        s = jnp.where(row >= col, s, LOW)
        top = jnp.broadcast_to(jnp.max(s, axis=1, keepdims=True), (TOK, HEAD))
        p = jnp.exp2(s - wide(top, TOK // HEAD)).astype(BF16)
        a[h] = plain(p, lv[...])
        m[h] = top


def chip_kernel(me_ref, c_ref, q0, q1, blk, m0i, a0i, m0, a0, m1, a1, kk, vv):
    me = me_ref[0]
    c = c_ref[0]
    core = me % NC
    y = (me // NC) % NY
    m0[...] = m0i[...]
    a0[...] = a0i[...]
    m1[...] = jnp.full(m1.shape, LOW, F32)
    a1[...] = jnp.zeros(a1.shape, F32)
    attend_set(me, core, [y], c, q0, blk, kk, vv, m0, a0)
    attend_set(me, 1 - core, [y], c, q1, blk, kk, vv, m1, a1)


def ring_kernel(step, me_ref, c_ref, q0, q1, fwd, bwd, m0i, a0i, m1i, a1i, m0, a0, m1, a1, blocks, kk, vv):
    me = me_ref[0]
    c = c_ref[0]
    y = (me // NC) % NY
    m0[...] = m0i[...]
    a0[...] = a0i[...]
    m1[...] = m1i[...]
    a1[...] = a1i[...]
    blocks[0:MSG, :] = fwd[...]
    blocks[MSG : 2 * MSG, :] = bwd[...]
    key_ys = [(y + NY - step) % NY, (y + step) % NY]
    attend_both(me, key_ys, c, ((q0, m0, a0), (q1, m1, a1)), blocks, kk, vv)


def last_kernel(other, me_ref, c_ref, q, blk, mi, ai, *rest):
    if other:
        out, m, a, kk, vv = rest
    else:
        m, a, kk, vv = rest
    me = me_ref[0]
    core = me % NC
    y = (me // NC) % NY
    m[...] = mi[...]
    a[...] = ai[...]
    key_ys = [(y + NY // 2) % NY]
    attend_set(me, 1 - core if other else core, key_ys, c_ref[0], q, blk, kk, vv, m, a)
    if other:
        lane = lax.broadcasted_iota(jnp.int32, (TOK, HEAD), 1)
        for h in range(HEADS):
            total = a[h][:, HEAD:]
            some = total > 0.0
            safe = jnp.where(some, total, 1.0)
            out[h, :, 0:HEAD] = (a[h][:, :HEAD] / safe).astype(BF16)
            lse = jnp.where(some, m[h] + jnp.log2(safe), LOW)
            hi = lse.astype(BF16).astype(F32)
            mid = (lse - hi).astype(BF16).astype(F32)
            low = lse - hi - mid
            parts = jnp.where(lane == 0, hi, jnp.where(lane == 1, mid, low))
            out[h, :, HEAD : 2 * HEAD] = parts.astype(BF16)


def project(att, w, half, j, cols):
    return plain(att[...], w[:, pl.ds(pl.multiple_of((half * NX + j) * cols, cols), cols)]).astype(BF16)


def merge_kernel(tp_ref, m, a, got, w, att, there):
    for h in range(HEADS):
        parts = got[h][:, HEAD:].astype(F32)
        lse = (parts[:, 0:1] + parts[:, 1:2]) + parts[:, 2:3]
        mine = m[h]
        top = jnp.maximum(mine, lse)
        w0 = jnp.exp2(mine - top)
        w1 = jnp.exp2(lse - top)
        acc = a[h][:, :HEAD] * w0 + got[h][:, :HEAD].astype(F32) * w1
        total = a[h][:, HEAD:] * w0 + w1
        att[:, h * HEAD : (h + 1) * HEAD] = (acc / total).astype(BF16)
    for j in range(NX):
        there[j] = project(att, w, 1 - tp_ref[0] // NX, j, there.shape[2])


def own_kernel(tp_ref, att, w, *outs):
    x, half = tp_ref[0] % NX, tp_ref[0] // NX
    for k, out in enumerate(outs):
        out[...] = project(att, w, half, (x + k) % NX, out.shape[1])


def sum_kernel(parts, out):
    total = parts[0].astype(F32)
    for j in range(1, NX):
        total += parts[j].astype(F32)
    out[...] = total.astype(BF16)


def choose_kernel(me_ref, here, there, out):
    last = me_ref[0] == NZ * NY * NC - 1

    @pl.when(last)
    def _():
        out[...] = there[...]

    @pl.when(jnp.logical_not(last))
    def _():
        out[...] = here[...]


def square_kernel(*refs):
    *parts, out, squares = refs
    total = parts[0][...].astype(F32)
    for part in parts[1:]:
        total += part[...].astype(F32)
    out[...] = total
    ones = jnp.ones((8, total.shape[1]), F32)
    sums = lax.dot_general(
        ones,
        total * total,
        (((1,), (1,)), ((), ())),
        precision=lax.Precision.HIGHEST,
        preferred_element_type=F32,
    )
    for j in range(NX * NH):
        squares[j] = sums


def norm_kernel(features, projected, squares, gain, out):
    total = squares[0]
    for j in range(1, NX * NH):
        total += squares[j]
    scale = lax.rsqrt(jnp.transpose(total)[:, 0:1] / features + 1e-05)
    out[...] = (projected[...] * scale * gain[...]).astype(BF16)


def params(mib=20):
    return pltpu.CompilerParams(vmem_limit_bytes=mib << 20)


def scratch(n):
    return [pltpu.VMEM((n * BLOCK, HEAD), BF16), pltpu.VMEM((n * BLOCK, 2 * HEAD), BF16)]


def cost(keys, sets):
    rows = HEADS * TOK * sets
    return pl.CostEstimate(
        flops=rows * keys * HEAD * 20, bytes_accessed=4 << 20, transcendentals=rows * keys
    )


def shards(queries, keys, values, key_head_scale, retained, out_weight, norm_gain):
    me = lax.axis_index("seq").astype(jnp.int32)
    tp = lax.axis_index("tp").astype(jnp.int32)
    z = me // (NC * NY)
    me_s = me.reshape(1)
    tp_s = tp.reshape(1)
    c = key_head_scale * (LOG2E / math.sqrt(HEAD))

    row = retained[0, 0] * BLOCK
    own = jnp.concatenate(
        [lax.dynamic_slice_in_dim(part, row, BLOCK, 0) for part in (keys, values)], 0
    )
    planes = [[sid(z_, y_, c_) for z_ in range(NZ)] for y_ in range(NY) for c_ in range(NC)]
    stack = lax.all_to_all(
        jnp.broadcast_to(own, (NZ, SLOT, HEAD)), "seq", 0, 0, axis_index_groups=planes
    )
    holders = [sid(z_, NY - 1, 1) for z_ in range(NZ)]
    anchor = jnp.concatenate([keys[:BLOCK], values[:BLOCK]], 0)
    far = lax.ppermute(anchor, "seq", [(0, holders[3])])
    other_queries = lax.ppermute(queries, "seq", [(sid(*s), sid(s[0], s[1], 1 - s[2])) for s in PLACES])
    anchor = pl.pallas_call(
        choose_kernel,
        out_shape=jax.ShapeDtypeStruct((SLOT, HEAD), BF16),
        in_specs=[SMEM] + [VMEM] * 2,
        out_specs=VMEM,
        compiler_params=params(),
        cost_estimate=pl.CostEstimate(flops=1 << 33, bytes_accessed=1 << 17, transcendentals=0),
        name="choose_anchor",
    )(me_s, anchor, far)
    near = lax.ppermute(anchor, "seq", [(0, holders[1]), (holders[3], holders[2])])
    placed = jnp.where(jnp.logical_or(me == holders[1], me == holders[2]), near, anchor)
    holds = jnp.where(z == 0, me == 0, me % (NY * NC) == NY * NC - 1)
    block = jnp.concatenate(
        [stack[: NZ - 1].reshape(MSG - SLOT, HEAD), jnp.where(holds, placed, stack[NZ - 1])], 0
    )

    fwd = [lax.ppermute(block, "seq", y_perm(1))]
    bwd = [lax.ppermute(block, "seq", y_perm(-1))]
    for _ in range(2):
        fwd.append(lax.ppermute(fwd[-1], "seq", y_perm(1)))
        bwd.append(lax.ppermute(bwd[-1], "seq", y_perm(-1)))
    up_pairs = [(sid(z_, y_, c_), sid(z_, y_ + 1, c_)) for z_, y_, c_ in PLACES if y_ % 2 == 0]
    to_odd = lax.ppermute(fwd[-1], "seq", up_pairs)
    to_even = lax.ppermute(bwd[-1], "seq", [(b, a) for a, b in up_pairs])
    half = jnp.where(me // NC % 2 == 0, to_even, to_odd)

    state_shapes = [M_SHAPE, ACC_SHAPE, M_SHAPE, ACC_SHAPE]
    m0, a0 = pl.pallas_call(
        local_kernel,
        out_shape=[M_SHAPE, ACC_SHAPE],
        in_specs=[SMEM] + [VMEM] * 3,
        out_specs=[VMEM] * 2,
        scratch_shapes=[pltpu.VMEM((TOK, 2 * HEAD), BF16)],
        compiler_params=params(),
        cost_estimate=cost(512, 1),
        name="attend_local",
    )(c, queries, keys, values)
    state = pl.pallas_call(
        chip_kernel,
        out_shape=state_shapes,
        in_specs=[SMEM, SMEM] + [VMEM] * 5,
        out_specs=[VMEM] * 4,
        scratch_shapes=scratch(4),
        input_output_aliases={5: 0, 6: 1},
        compiler_params=params(),
        cost_estimate=cost(512, 2),
        name="attend_own_chip",
    )(me_s, c, queries, other_queries, block, m0, a0)
    for step in range(1, 4):
        state = pl.pallas_call(
            functools.partial(ring_kernel, step),
            out_shape=state_shapes,
            in_specs=[SMEM, SMEM] + [VMEM] * 8,
            out_specs=[VMEM] * 4,
            scratch_shapes=[pltpu.VMEM((2 * MSG, HEAD), BF16)] + scratch(8),
            input_output_aliases={6: 0, 7: 1, 8: 2, 9: 3},
            compiler_params=params(),
            cost_estimate=cost(1024, 2),
            name="attend_ring",
        )(me_s, c, queries, other_queries, fwd[step - 1], bwd[step - 1], *state)
    m0, a0, m1, a1 = state
    message, _, _ = pl.pallas_call(
        functools.partial(last_kernel, True),
        out_shape=[jax.ShapeDtypeStruct((HEADS, TOK, 2 * HEAD), BF16), M_SHAPE, ACC_SHAPE],
        in_specs=[SMEM, SMEM] + [VMEM] * 4,
        out_specs=[VMEM] * 3,
        scratch_shapes=scratch(4),
        input_output_aliases={4: 1, 5: 2},
        compiler_params=params(),
        cost_estimate=cost(512, 1),
        name="attend_last_other",
    )(me_s, c, other_queries, half, m1, a1)
    got = lax.ppermute(message, "seq", [(sid(*s), sid(s[0], s[1], 1 - s[2])) for s in PLACES])
    m0, a0 = pl.pallas_call(
        functools.partial(last_kernel, False),
        out_shape=[M_SHAPE, ACC_SHAPE],
        in_specs=[SMEM, SMEM] + [VMEM] * 4,
        out_specs=[VMEM] * 2,
        scratch_shapes=scratch(4),
        input_output_aliases={4: 0, 5: 1},
        compiler_params=params(),
        cost_estimate=cost(512, 1),
        name="attend_last_own",
    )(me_s, c, queries, half, m0, a0)

    wide_cols = out_weight.shape[1] // (NX * NH)

    block_shape = jax.ShapeDtypeStruct((TOK, wide_cols), BF16)
    att, there = pl.pallas_call(
        merge_kernel,
        out_shape=[
            jax.ShapeDtypeStruct((TOK, HEADS * HEAD), BF16),
            jax.ShapeDtypeStruct((NX, TOK, wide_cols), BF16),
        ],
        in_specs=[SMEM] + [VMEM] * 4,
        out_specs=[VMEM] * 2,
        compiler_params=params(),
        cost_estimate=pl.CostEstimate(flops=1 << 31, bytes_accessed=8 << 20, transcendentals=1 << 18),
        name="merge_project",
    )(tp_s, m0, a0, got, out_weight)
    rows = [[h * NX + x for x in range(NX)] for h in range(NH)]
    swap = [(i, (i + NX) % (NX * NH)) for i in range(NX * NH)]
    there = lax.all_to_all(there, "tp", 0, 0, axis_index_groups=rows)
    here = pl.pallas_call(
        own_kernel,
        out_shape=[block_shape] * NX,
        in_specs=[SMEM] + [VMEM] * 2,
        out_specs=[VMEM] * NX,
        compiler_params=params(),
        cost_estimate=pl.CostEstimate(flops=1 << 31, bytes_accessed=2 << 20, transcendentals=0),
        name="project_own_half",
    )(tp_s, att, out_weight)
    parts = [here[0]] + [
        lax.ppermute(here[k], "tp", [(i, i // NX * NX + (i + k) % NX) for i in range(NX * NH)])
        for k in range(1, NX)
    ]
    there = pl.pallas_call(
        sum_kernel,
        out_shape=block_shape,
        in_specs=[VMEM],
        out_specs=VMEM,
        compiler_params=params(),
        name="sum_other_half",
    )(there)
    parts.append(lax.ppermute(there, "tp", swap))
    projected, squares = pl.pallas_call(
        square_kernel,
        out_shape=[
            jax.ShapeDtypeStruct((TOK, wide_cols), F32),
            jax.ShapeDtypeStruct((NX * NH, 8, TOK), F32),
        ],
        in_specs=[VMEM] * (NX + 1),
        out_specs=[VMEM] * 2,
        compiler_params=params(),
        name="sum_and_square",
    )(*parts)
    squares = lax.all_to_all(squares, "tp", 0, 0)
    return pl.pallas_call(
        functools.partial(norm_kernel, out_weight.shape[1]),
        out_shape=jax.ShapeDtypeStruct((TOK, wide_cols), BF16),
        in_specs=[VMEM] * 3,
        out_specs=VMEM,
        compiler_params=params(),
        name="normalize",
    )(projected, squares, norm_gain.reshape(1, wide_cols))


def solution(mesh):
    return jax.shard_map(
        shards,
        mesh=mesh,
        in_specs=(
            P("seq", "tp"),
            P("seq", "tp"),
            P("seq", "tp"),
            P("tp"),
            P("seq", None),
            P("tp", None),
            P("tp"),
        ),
        out_specs=P("seq", "tp"),
        check_vma=False,
    )
```
